32 devices in a mesh: section: 2 (over core), dp: 4 (over z), seq: 4 (over y, x).
Axes of the slice: x: 2, y: 2, z: 4, core: 2. Of those that a mesh axis runs over, the one named last changes fastest.
Arguments:
- inputs: bfloat16 [12, 1024, 1600], P('dp', 'seq'), may hold values from -6 to 6
- cotangent: bfloat16 [12, 1024, 1600], P('dp', 'seq'), may hold values from -6 to 6
- lengths: int32 [12], replicated, may hold values from 256 to 1024, as said below
- dealing: int32 [12], replicated, may hold values from 0 to 11, as said below
- query_key_value_weight: bfloat16 [2, 1600, 4800], P('section', ('dp', 'seq')), may hold values from -0.15625 to 0.15625
- b_qv: bfloat16 [2, 3200], P('section', ('dp', 'seq')), may hold values from -3 to 3
- attention_out_weight: bfloat16 [2, 1600, 1600], P('section', ('dp', 'seq')), may hold values from -0.625 to 0.625
- attention_out_bias: bfloat16 [2, 1600], P('section', ('dp', 'seq')), may hold values from -3 to 3
- up_weight: bfloat16 [2, 1600, 6400], P('section', ('dp', 'seq')), may hold values from -0.15625 to 0.15625
- up_bias: bfloat16 [2, 6400], P('section', ('dp', 'seq')), may hold values from -3 to 3
- down_weight: bfloat16 [2, 6400, 1600], P('section', ('dp', 'seq')), may hold values from -0.078125 to 0.078125
- down_bias: bfloat16 [2, 1600], P('section', ('dp', 'seq')), may hold values from -3 to 3
- gain_one: bfloat16 [2, 1600], P('section', ('dp', 'seq')), may hold values from 0.099609375 to 1.8984375
- shift_one: bfloat16 [2, 1600], P('section', ('dp', 'seq')), may hold values from -3 to 3
- gain_two: bfloat16 [2, 1600], P('section', ('dp', 'seq')), may hold values from 0.099609375 to 1.8984375
- shift_two: bfloat16 [2, 1600], P('section', ('dp', 'seq')), may hold values from -3 to 3
Outputs:
- acts: bfloat16 [2, 12, 1024, 1600], P('section', 'dp', 'seq')
- input_grad: bfloat16 [2, 12, 1024, 1600], P('section', 'dp', 'seq')
- grad_w_qkv: float32 [2, 1600, 4800], P('section', ('dp', 'seq'))
- grad_b_qv: float32 [2, 3200], P('section', ('dp', 'seq'))
- grad_w_out: float32 [2, 1600, 1600], P('section', ('dp', 'seq'))
- grad_b_out: float32 [2, 1600], P('section', ('dp', 'seq'))
- grad_w_up: float32 [2, 1600, 6400], P('section', ('dp', 'seq'))
- grad_b_up: float32 [2, 6400], P('section', ('dp', 'seq'))
- grad_w_down: float32 [2, 6400, 1600], P('section', ('dp', 'seq'))
- grad_b_down: float32 [2, 1600], P('section', ('dp', 'seq'))
- grad_gain_one: float32 [2, 1600], P('section', ('dp', 'seq'))
- grad_shift_one: float32 [2, 1600], P('section', ('dp', 'seq'))
- grad_gain_two: float32 [2, 1600], P('section', ('dp', 'seq'))
- grad_shift_two: float32 [2, 1600], P('section', ('dp', 'seq'))
The draws below stay inside these ranges and needn't reach their ends.
Inputs may be any that keep to these rules, and one draw needn't show every extreme that they name: dealing is a permutation; the 3 sequences of one group come from 3 different aligned blocks of 3 input sequences, and the sequences of one block go to different groups. `lengths`: every group takes one sequence of length 1024.
All inputs are finite; a program needn't handle non-finite values.
Results may differ from the reference program's by a relative error of at most 0.018.
Values may be sent and summed in bfloat16 or wider, within the bound.
No kernel may reach another device: no remote copies, remote signals or barrier semaphores. Data moves between devices by JAX's collectives and lax.ppermute only.
A program may use at most 448 MiB of HBM per device.

```python
from functools import partial
import jax
import jax.numpy as jnp
from jax import lax

D = 1600
H = 25
HD = 64
FF = 6400
LMAX = 1024
MICRO = 3
SEQS = 12


def shuffle_one(subkey):
    return jax.random.permutation(subkey, MICRO)


def deal_groups(key):
    group_count = SEQS // MICRO
    offsets = jax.random.permutation(jax.random.fold_in(key, 101), group_count)[:MICRO]
    inner = jax.vmap(shuffle_one)(jax.random.split(jax.random.fold_in(key, 102), group_count))
    group_ids = jnp.arange(group_count, dtype=jnp.int32)
    source = (group_ids[:, None] + offsets[None, :]) % group_count
    within = inner[source, jnp.arange(MICRO, dtype=jnp.int32)[None, :]]
    return (source * MICRO + within).reshape(-1).astype(jnp.int32)


def draw_dealing(key, part):
    dealing = deal_groups(key)
    return dealing


def draw_lengths(key, part):
    dealing = deal_groups(key)
    key = jax.random.fold_in(key, 5)
    group_count = SEQS // MICRO
    drawn = jax.random.randint(jax.random.fold_in(key, 1), (SEQS,), LMAX // 4, LMAX + 1)
    chosen = jax.random.randint(jax.random.fold_in(key, 2), (group_count,), 0, MICRO)
    longest = dealing.reshape(group_count, MICRO)[jnp.arange(group_count), chosen]
    return drawn.at[longest].set(LMAX).astype(jnp.int32)


def block_levels(rng, dims, cuts, low, largest):
    factor_of = 1.0
    for dim, parts in cuts:
        heights = jax.random.uniform(jax.random.fold_in(jax.random.fold_in(rng, 6), dim), (parts,), jnp.float32, low / len(cuts), largest / len(cuts))
        factor_of = factor_of * jnp.repeat(jnp.exp(heights), dims[dim] // parts).reshape((-1,) + (1,) * (len(dims) - 1 - dim))
    return factor_of


def bell_draw(stream_key, shape, spread, most, pieces=(), kind=jnp.bfloat16):
    values = spread * jax.random.normal(stream_key, shape, jnp.float32)
    if pieces:
        values = values * block_levels(stream_key, shape, pieces, -0.22, 0.18)
    return jnp.clip(values, -most, most).astype(kind)


def setup_inputs(seed: int = 0) -> dict:
    splits = jax.random.split(jax.random.key(seed), 17)
    inputs = bell_draw(splits[0], (SEQS, LMAX, D), 1.0, 6.0, ((0, 4), (1, 4)))
    cotangent = bell_draw(splits[1], (SEQS, LMAX, D), 1.0, 6.0, ((0, 4), (1, 4)))
    lengths = draw_lengths(jax.random.fold_in(splits[16], 71), 0)
    dealing = draw_dealing(jax.random.fold_in(splits[16], 71), 0)
    query_key_value_weight = bell_draw(splits[4], (2, D, 3 * D), D ** -0.5, 0.15625, ((0, 2), (1, 16)))
    b_qv = bell_draw(splits[5], (2, 2 * D), 0.5, 3.0, ((0, 2), (1, 16)))
    attention_out_weight = bell_draw(splits[6], (2, D, D), (D // 16) ** -0.5, 0.625, ((0, 2), (1, 16)))
    attention_out_bias = bell_draw(splits[7], (2, D), 0.5, 3.0, ((0, 2), (1, 16)))
    up_weight = bell_draw(splits[8], (2, D, FF), D ** -0.5, 0.15625, ((0, 2), (1, 16)))
    up_bias = bell_draw(splits[9], (2, FF), 0.5, 3.0, ((0, 2), (1, 16)))
    down_weight = bell_draw(splits[10], (2, FF, D), FF ** -0.5, 0.078125, ((0, 2), (1, 16)))
    down_bias = bell_draw(splits[11], (2, D), 0.5, 3.0, ((0, 2), (1, 16)))
    gain_one = jnp.clip(1.0 + 0.18 * jax.random.normal(splits[12], (2, D), jnp.float32), 0.099609375, 1.8984375).astype(jnp.bfloat16)
    shift_one = bell_draw(splits[13], (2, D), 0.5, 3.0, ((0, 2), (1, 16)))
    gain_two = jnp.clip(1.0 + 0.18 * jax.random.normal(splits[14], (2, D), jnp.float32), 0.099609375, 1.8984375).astype(jnp.bfloat16)
    shift_two = bell_draw(splits[15], (2, D), 0.5, 3.0, ((0, 2), (1, 16)))
    return {"inputs": inputs, "cotangent": cotangent, "lengths": lengths, "dealing": dealing, "query_key_value_weight": query_key_value_weight, "b_qv": b_qv, "attention_out_weight": attention_out_weight, "attention_out_bias": attention_out_bias, "up_weight": up_weight, "up_bias": up_bias, "down_weight": down_weight, "down_bias": down_bias, "gain_one": gain_one, "shift_one": shift_one, "gain_two": gain_two, "shift_two": shift_two}


@jax.custom_vjp
def low(v):
    return lax.optimization_barrier(v.astype(jnp.bfloat16)).astype(jnp.float32)

@jax.custom_vjp
def low_back(v):
    return v

def low_keep(v):
    return (low(v), None)

def low_pass(kept, grad):
    return (grad,)

def back_keep(v):
    return (v, None)

def back_low(kept, grad):
    return (low(grad),)
low.defvjp(low_keep, low_pass)
low_back.defvjp(back_keep, back_low)
highest_precision = lax.Precision.HIGHEST

def normalize(row_block, gain_vec, shift_vec):
    average = lax.optimization_barrier(jnp.mean(row_block, axis=-1, keepdims=True))
    centered = row_block - average
    variance = lax.optimization_barrier(jnp.mean(centered * centered, axis=-1, keepdims=True))
    return centered * lax.rsqrt(variance + 1e-05) * gain_vec + shift_vec

def attend_one(packed):
    queries, key_rows, value_rows, length = packed
    scores = jnp.einsum('qhd,khd->hqk', queries, key_rows, precision=highest_precision) * HD ** (-0.5)
    scores = low_back(scores)
    positions = jnp.arange(LMAX, dtype=jnp.int32)
    allowed = (positions[None, :] <= positions[:, None]) & (positions[None, :] < length)
    scores = jnp.where(allowed[None], scores, -1e+30)
    maxima = lax.optimization_barrier(jnp.max(scores, axis=-1, keepdims=True))
    weights = jnp.exp(scores - maxima)
    probabilities = low(weights / lax.optimization_barrier(jnp.sum(weights, axis=-1, keepdims=True)))
    return jnp.einsum('hqk,khd->qhd', probabilities, value_rows, precision=highest_precision)

def block_layer(row_block, params, lengths):
    query_key_value_weight, b_qv, attention_out_weight, attention_out_bias, up_weight, up_bias, down_weight, down_bias, gain_one, shift_one, gain_two, shift_two = params
    normalized_first = low(normalize(row_block, gain_one, shift_one))
    query_key_value_bias = jnp.concatenate([b_qv[:D], jnp.zeros((D,), jnp.float32), b_qv[D:]])
    attention_projected = jnp.einsum('kqf,fj->kqj', normalized_first, query_key_value_weight, precision=highest_precision) + query_key_value_bias
    attention_projected = low(low_back(attention_projected))
    queries = attention_projected[:, :, :D].reshape(SEQS, LMAX, H, HD)
    key_rows = attention_projected[:, :, D:2 * D].reshape(SEQS, LMAX, H, HD)
    value_rows = attention_projected[:, :, 2 * D:].reshape(SEQS, LMAX, H, HD)
    attention_result = lax.map(jax.checkpoint(attend_one), (queries, key_rows, value_rows, lengths))
    attention_result = low(low_back(attention_result.reshape(SEQS, LMAX, D)))
    residual_branch = low_back(jnp.einsum('kqf,fj->kqj', attention_result, attention_out_weight, precision=highest_precision) + attention_out_bias)
    middle = row_block + residual_branch
    normalized_second = low(normalize(middle, gain_two, shift_two))
    up_projected = low_back(jnp.einsum('boy,yv->bov', normalized_second, up_weight, precision=highest_precision) + up_bias)
    hidden_units = low(jax.nn.gelu(up_projected, approximate=True))
    down_projected = low_back(jnp.einsum('erb,bx->erx', hidden_units, down_weight, precision=highest_precision) + down_bias)
    return middle + down_projected

def forward(start_rows, probe_rows, params_one, params_two, lengths=None):
    out_one = block_layer(start_rows, params_one, lengths)
    handed = low(low_back(out_one)) + probe_rows
    out_two = block_layer(handed, params_two, lengths)
    return (out_one, out_two)

def reference(inputs, cotangent, lengths, dealing, query_key_value_weight, b_qv, attention_out_weight, attention_out_bias, up_weight, up_bias, down_weight, down_bias, gain_one, shift_one, gain_two, shift_two):
    params = tuple((weight.astype(jnp.float32) for weight in (query_key_value_weight, b_qv, attention_out_weight, attention_out_bias, up_weight, up_bias, down_weight, down_bias, gain_one, shift_one, gain_two, shift_two)))
    params_one = tuple((weight[0] for weight in params))
    params_two = tuple((weight[1] for weight in params))
    positions = jnp.arange(LMAX, dtype=jnp.int32)
    valid = (positions[None, :] < lengths[:, None]).astype(jnp.float32)
    masked_grad = cotangent.astype(jnp.float32) * valid[:, :, None]
    start_rows = inputs.astype(jnp.float32)
    probe_rows = jnp.zeros_like(start_rows)
    outcome, backward = jax.vjp(partial(forward, lengths=lengths), start_rows, probe_rows, params_one, params_two)
    grad_start, grad_probe, grads_one, grads_two = backward((jnp.zeros_like(outcome[0]), masked_grad))
    acts = jnp.stack([outcome[0], outcome[1]])[:, dealing].astype(jnp.bfloat16)
    input_grad = jnp.stack([grad_start, grad_probe]).astype(jnp.bfloat16)
    stacked = [jnp.stack([one_grad, two_grad]) for one_grad, two_grad in zip(grads_one, grads_two)]
    return (acts, input_grad, stacked[0], stacked[1], stacked[2], stacked[3], stacked[4], stacked[5], stacked[6], stacked[7], stacked[8], stacked[9], stacked[10], stacked[11])
```

```python
import functools

import jax
import jax.numpy as jnp
from jax import lax
from jax.experimental import pallas as pl
from jax.experimental.pallas import tpu as pltpu
from jax.sharding import PartitionSpec as P

H = 25
HD = 64
QUARTERS = 4
HL = -(-H // QUARTERS)
HSTEP = (H - HL) // (QUARTERS - 1)
PAIRS = -(-HL // 2)
QK_LANES = HL * 2 * HD
V_LANES = PAIRS * 2 * HD
P_LANES = QK_LANES + V_LANES
ROW_BLOCK = 256
F32 = jnp.float32
BF16 = jnp.bfloat16


def round_up(value, by):
    return -(-value // by) * by


def masked_probs(q, k, first, length):
    scores = lax.dot_general(q, k, (((1,), (1,)), ((), ())), preferred_element_type=F32)
    rows = first + lax.broadcasted_iota(jnp.int32, scores.shape, 0)
    cols = lax.broadcasted_iota(jnp.int32, scores.shape, 1)
    scores = jnp.where((cols <= rows) & (cols < length), scores, -1e30)
    top = jnp.max(scores, axis=1, keepdims=True)
    weights = jnp.exp(scores - top)
    return weights * (1.0 / jnp.sum(weights, axis=1, keepdims=True))


def attn_fwd_kernel(len_ref, qk_ref, v_ref, o_ref):
    total = qk_ref.shape[0]
    block = min(ROW_BLOCK, total)
    length = len_ref[0]
    lower = lax.broadcasted_iota(jnp.int32, (block, 2 * HD), 1) < HD

    def rows_of(i, both):
        first, end = i * block, (i + 1) * block
        parts = []
        for a in range(2 if both else 1):
            q = qk_ref[first:end, 2 * HD * a : 2 * HD * a + HD] * jnp.asarray(HD**-0.5, BF16)
            k = qk_ref[:end, 2 * HD * a + HD : 2 * HD * (a + 1)]
            probs = masked_probs(q, k, first, length).astype(BF16)
            parts.append(jnp.dot(probs, v_ref[:end, :], preferred_element_type=F32))
        upper = parts[1] if both else jnp.zeros_like(parts[0])
        o_ref[first:end, :] = jnp.where(lower, parts[0], upper).astype(BF16)

    if HL % 2 == 0:
        for i in range(total // block):
            rows_of(i, True)
        return
    last = pl.program_id(0) == PAIRS - 1

    @pl.when(jnp.logical_not(last))
    def _():
        for i in range(total // block):
            rows_of(i, True)

    @pl.when(last)
    def _():
        for i in range(total // block):
            rows_of(i, False)


def attn_forward(packed, length):
    total = packed.shape[0]
    return pl.pallas_call(
        attn_fwd_kernel,
        grid=(PAIRS,),
        in_specs=[
            pl.BlockSpec(memory_space=pltpu.SMEM),
            pl.BlockSpec((total, 4 * HD), lambda j: (0, j)),
            pl.BlockSpec((total, 2 * HD), lambda j: (0, j + QK_LANES // (2 * HD))),
        ],
        out_specs=pl.BlockSpec((total, 2 * HD), lambda j: (0, j)),
        out_shape=jax.ShapeDtypeStruct((total, V_LANES), BF16),
        compiler_params=pltpu.CompilerParams(vmem_limit_bytes=40 * 2**20),
        cost_estimate=pl.CostEstimate(
            flops=2 * 2 * HL * total * total * 256, bytes_accessed=4 * total * P_LANES, transcendentals=HL * total * total
        ),
        name="attn_fwd",
    )(length, packed, packed)


def attn_bwd_kernel(len_ref, qk_ref, v_ref, g_ref, out_ref, dk_ref, dv_ref):
    total = qk_ref.shape[0]
    block = min(ROW_BLOCK, total)
    length = len_ref[0]
    pair = pl.program_id(0)
    scale = jnp.asarray(HD**-0.5, BF16)
    lane = lax.broadcasted_iota(jnp.int32, (block, 2 * HD), 1)
    lane_all = lax.broadcasted_iota(jnp.int32, (total, 2 * HD), 1)

    def head(a):
        dk_ref[...] = jnp.zeros_like(dk_ref)
        mine = (lane < HD) if a == 0 else (lane >= HD)
        dq_parts = []
        for i in range(total // block):
            first, end = i * block, (i + 1) * block
            q = qk_ref[first:end, 2 * HD * a : 2 * HD * a + HD] * scale
            k = qk_ref[:end, 2 * HD * a + HD : 2 * HD * (a + 1)]
            g = g_ref[first:end, :]
            g_mine = jnp.where(mine, g, jnp.zeros_like(g))
            probs = masked_probs(q, k, first, length)
            gprobs = lax.dot_general(g_mine, v_ref[:end, :], (((1,), (1,)), ((), ())), preferred_element_type=F32)
            inner = jnp.sum(probs * gprobs, axis=1, keepdims=True)
            gscores = (probs * (gprobs - inner)).astype(BF16)
            dq_parts.append((jnp.dot(gscores, k, preferred_element_type=F32) * HD**-0.5).astype(BF16))
            dk_ref[:end, :] += lax.dot_general(gscores, q, (((0,), (0,)), ((), ())), preferred_element_type=F32)
            dv_ref[:end, :] += lax.dot_general(
                probs.astype(BF16), g_mine, (((0,), (0,)), ((), ())), preferred_element_type=F32
            )
        return jnp.concatenate([jnp.concatenate(dq_parts, axis=0), dk_ref[...].astype(BF16)], axis=1)

    dv_ref[...] = jnp.zeros_like(dv_ref)
    out_ref[:, pl.ds(pl.multiple_of(pair * 4 * HD, 2 * HD), 2 * HD)] = head(0)

    @pl.when(2 * pair + 1 < HL)
    def _():
        out_ref[:, pl.ds(pl.multiple_of(pair * 4 * HD + 2 * HD, 2 * HD), 2 * HD)] = head(1)

    out_ref[:, pl.ds(pl.multiple_of(QK_LANES + pair * 2 * HD, 2 * HD), 2 * HD)] = dv_ref[...].astype(BF16)


def attn_backward(packed, grad, length):
    total = packed.shape[0]
    return pl.pallas_call(
        attn_bwd_kernel,
        grid=(PAIRS,),
        in_specs=[
            pl.BlockSpec(memory_space=pltpu.SMEM),
            pl.BlockSpec((total, 4 * HD), lambda j: (0, j)),
            pl.BlockSpec((total, 2 * HD), lambda j: (0, j + QK_LANES // (2 * HD))),
            pl.BlockSpec((total, 2 * HD), lambda j: (0, j)),
        ],
        out_specs=pl.BlockSpec((total, P_LANES), lambda j: (0, 0)),
        out_shape=jax.ShapeDtypeStruct((total, P_LANES), BF16),
        scratch_shapes=[pltpu.VMEM((total, HD), F32), pltpu.VMEM((total, 2 * HD), F32)],
        compiler_params=pltpu.CompilerParams(vmem_limit_bytes=48 * 2**20),
        cost_estimate=pl.CostEstimate(
            flops=5 * 2 * HL * total * total * 256, bytes_accessed=6 * total * P_LANES, transcendentals=HL * total * total
        ),
        name="attn_bwd",
    )(length, packed, packed, grad)


def flip(value, axis, bit):
    count = lax.axis_size(axis)
    return lax.ppermute(value, axis, [(i, i ^ (1 << bit)) for i in range(count)])


def bit_of(axis, bit):
    return (lax.axis_index(axis) >> bit) & 1


def bits_in(axis):
    return (lax.axis_size(axis) - 1).bit_length()


def group_bits():
    z = [("dp", b) for b in reversed(range(bits_in("dp")))]
    y = [("seq", b) for b in reversed(range(1, bits_in("seq")))]
    return z, y


X_BIT = ("seq", 0)


def swap_cores(value):
    return lax.ppermute(value, "section", [(0, 1), (1, 0)])


def in_core_order(mine, other, axis):
    core = lax.axis_index("section")
    low = jnp.where(core == 0, mine, other)
    high = jnp.where(core == 0, other, mine)
    return jnp.concatenate([low, high], axis=axis)


def gather_step(value, bit, axis):
    other = flip(value, *bit)
    mine_low = bit_of(*bit) == 0
    low = jnp.where(mine_low, value, other)
    high = jnp.where(mine_low, other, value)
    return jnp.concatenate([low, high], axis=axis)


def gather_blocks(value, order, places):
    value = value.reshape((1,) * len(places) + value.shape)
    before_last = value
    for bit in order:
        before_last = value
        value = gather_step(value, bit, places.index(bit))
    return value.reshape((-1,) + value.shape[len(places) :]), before_last


def scatter_step(value, bit, axis):
    mine_low = bit_of(*bit) == 0
    low = lax.slice_in_dim(value, 0, 1, axis=axis)
    high = lax.slice_in_dim(value, 1, 2, axis=axis)
    keep = jnp.where(mine_low, low, high)
    send = jnp.where(mine_low, high, low)
    return (keep.astype(F32) + flip(send, *bit).astype(F32)).astype(BF16)


def scatter_blocks(value, order, places):
    value = value.reshape((2,) * len(places) + value.shape[1:])
    for bit in order:
        value = scatter_step(value, bit, places.index(bit))
    return value.reshape(value.shape[len(places) :])


def after(value, token):
    return lax.optimization_barrier((value, token))[0]


def rows_of_both(own):
    return in_core_order(own, swap_cores(own), 0)


def summed_rows(partial):
    half = partial.shape[0] // 2
    core = lax.axis_index("section")
    low, high = partial[:half], partial[half:]
    own = jnp.where(core == 0, low, high)
    other = jnp.where(core == 0, high, low)
    chip = (own.astype(F32) + swap_cores(other).astype(F32)).astype(BF16)
    return chip.astype(F32) + flip(chip, *X_BIT).astype(F32)


def dot(a, b):
    return jnp.dot(a, b, preferred_element_type=F32)


def dot_t(a, b):
    return lax.dot_general(a, b, (((1,), (1,)), ((), ())), preferred_element_type=F32)


def dot_0(a, b):
    return lax.dot_general(a, b, (((0,), (0,)), ((), ())), preferred_element_type=F32)


def gelu_parts(u):
    t = jnp.tanh(0.7978845608 * (u + 0.044715 * u * u * u))
    return t


def gelu(u):
    return 0.5 * u * (1.0 + gelu_parts(u))


def gelu_slope(u):
    t = gelu_parts(u)
    return 0.5 * (1.0 + t) + 0.5 * u * (1.0 - t * t) * 0.7978845608 * (1.0 + 3 * 0.044715 * u * u)


def norm_stats(rows, mask, width):
    average = jnp.sum(rows, axis=-1, keepdims=True) / width
    centered = (rows - average) * mask
    variance = jnp.sum(centered * centered, axis=-1, keepdims=True) / width
    scale = lax.rsqrt(variance + 1e-05)
    return centered * scale, scale


def norm_back(grad, rows, gain, mask, width):
    hat, scale = norm_stats(rows, mask, width)
    inner = grad * gain
    mean_one = jnp.sum(inner, axis=-1, keepdims=True) / width
    mean_two = jnp.sum(inner * hat, axis=-1, keepdims=True) / width
    back = scale * (inner - mean_one - hat * mean_two) * mask
    return back, jnp.sum(grad * hat, axis=0), jnp.sum(grad * mask, axis=0)


def layer_forward(rows, w, length, mask, width):
    hat, _ = norm_stats(rows, mask, width)
    normed = rows_of_both((hat * w["gain_one"] + w["shift_one"]).astype(BF16))
    packed = (dot(normed, w["qkv"]) + w["qkv_bias"]).astype(BF16)
    attended = attn_forward(packed, length)
    branch = summed_rows(dot(attended, w["out"]).astype(BF16))
    middle = rows + branch + w["out_bias"]
    hat_two, _ = norm_stats(middle, mask, width)
    normed_two = rows_of_both((hat_two * w["gain_two"] + w["shift_two"]).astype(BF16))
    upward = dot(normed_two, w["up"]) + w["up_bias"]
    hidden = gelu(upward).astype(BF16)
    branch_two = summed_rows(dot(hidden, w["down"]).astype(BF16))
    result = middle + branch_two + w["down_bias"]
    stored = (rows, normed, packed, attended, middle, normed_two, upward.astype(BF16), hidden)
    return result, stored


def ffn_backward(grad_out, stored, w, mask, width):
    rows, normed, packed, attended, middle, normed_two, upward, hidden = stored
    grad_down = grad_out.astype(BF16)
    b_down = jnp.sum(grad_down.astype(F32), axis=0)
    grad_down = rows_of_both(grad_down)
    grad_up = (dot_t(grad_down, w["down"]) * gelu_slope(upward.astype(F32))).astype(BF16)
    b_up = jnp.sum(grad_up.astype(F32), axis=0)
    grad_normed = summed_rows(dot_t(grad_up, w["up"]).astype(BF16))
    back, gain, shift = norm_back(grad_normed, middle, w["gain_two"], mask, width)
    grad_middle = grad_out + back
    small = {"down_bias": b_down, "up_bias": b_up, "gain_two": gain, "shift_two": shift}
    return grad_middle, small, {"down": (hidden, grad_down), "up": (normed_two, grad_up)}


def attn_layer_backward(grad_middle, stored, w, length, mask, width):
    rows, normed, packed, attended, middle, normed_two, upward, hidden = stored
    grad_branch = grad_middle.astype(BF16)
    b_out = jnp.sum(grad_branch.astype(F32), axis=0)
    grad_branch = rows_of_both(grad_branch)
    grad_attended = dot_t(grad_branch, w["out"]).astype(BF16)
    grad_packed = attn_backward(packed, grad_attended, length)
    b_packed = jnp.sum(grad_packed.astype(F32), axis=0)
    grad_normed = summed_rows(dot_t(grad_packed, w["qkv"]).astype(BF16))
    back, gain, shift = norm_back(grad_normed, rows.astype(F32), w["gain_one"], mask, width)
    small = {"out_bias": b_out, "packed": b_packed, "gain_one": gain, "shift_one": shift}
    return grad_middle + back, small, {"out": (attended, grad_branch), "qkv": (normed, grad_packed)}


SMALL = ("b_qv", "out_bias", "up_bias", "down_bias", "gain_one", "shift_one", "gain_two", "shift_two")


def per_device(
    inputs,
    cotangent,
    lengths,
    dealing,
    query_key_value_weight,
    b_qv,
    attention_out_weight,
    attention_out_bias,
    up_weight,
    up_bias,
    down_weight,
    down_bias,
    gain_one,
    shift_one,
    gain_two,
    shift_two,
):
    micro, block_rows, width = inputs.shape
    dp_count, seq_count = lax.axis_size("dp"), lax.axis_size("seq")
    chips = dp_count * seq_count
    dp_index, seq_index, core = lax.axis_index("dp"), lax.axis_index("seq"), lax.axis_index("section")
    x_index, y_index = seq_index & 1, seq_index >> 1
    groups = seq_count // 2
    rounds = -(-micro // groups)
    half_blocks = seq_count // 2
    half_rows = half_blocks * block_rows
    part = query_key_value_weight.shape[1]
    part_pad = round_up(part + 1, 8)
    width_pad = chips * part_pad
    hid = down_weight.shape[1] // 2
    hid_pad = round_up(hid, 8)
    all_groups = dp_count * groups
    z_bits, y_bits = group_bits()
    places = z_bits + y_bits
    places_all = places + [X_BIT]
    quarter = 2 * x_index + core

    lane = lax.broadcasted_iota(jnp.int32, (1, width_pad), 1)
    mask = (lane % part_pad < part).astype(F32)
    plain = lax.broadcasted_iota(jnp.int32, (width, width_pad), 0)
    padded = lax.broadcasted_iota(jnp.int32, (width, width_pad), 1)
    spread = (padded == plain // part * part_pad + plain % part).astype(BF16)

    def widen(value):
        return lax.dot_general(
            value, spread, (((value.ndim - 1,), (0,)), ((), ())), preferred_element_type=F32
        ).astype(BF16)

    def narrow(value):
        return lax.dot_general(
            value.astype(BF16), spread, (((value.ndim - 1,), (1,)), ((), ())), preferred_element_type=F32
        )

    def pad_rows(value, rows):
        return jnp.pad(value, ((0, rows - value.shape[0]), (0, 0)))

    small_in = dict(
        zip(SMALL, (b_qv, attention_out_bias, up_bias, down_bias, gain_one, shift_one, gain_two, shift_two))
    )
    small_sizes = {name: value.shape[1] for name, value in small_in.items()}
    small_row = jnp.concatenate([small_in[name][0] for name in SMALL])
    small_total = small_row.shape[0]

    shard = query_key_value_weight[0].reshape(part, 3, H, HD)

    def qkv_piece(q):
        from_head = HSTEP * q
        heads = shard[:, :, from_head : from_head + HL]
        qk = jnp.concatenate([heads[:, 0], heads[:, 1]], axis=-1).reshape(part, QK_LANES)
        v = heads[:, 2].reshape(part, HL * HD)
        body = jnp.concatenate([qk, v, jnp.zeros((part, V_LANES - HL * HD), BF16)], axis=1)
        row = jnp.pad(small_row, (0, P_LANES - small_total))[None]
        return pad_rows(jnp.concatenate([body, row], axis=0), part_pad)

    up_shard = up_weight[0].reshape(part, all_groups, 2, 2, hid)

    def up_piece(q):
        body = up_shard[:, :, q // 2, q % 2]
        body = jnp.pad(body, ((0, 0), (0, 0), (0, hid_pad - hid))).reshape(part, all_groups * hid_pad)
        return pad_rows(body, part_pad)

    qkv_pieces = jnp.stack([jnp.stack([qkv_piece(2 * x + c) for x in range(2)]) for c in range(2)])
    up_pieces = jnp.stack([jnp.stack([up_piece(2 * x + c) for x in range(2)]) for c in range(2)])
    out_wide = pad_rows(widen(attention_out_weight[0]), part_pad)
    out_pieces = jnp.stack([out_wide[:, : width_pad // 2], out_wide[:, width_pad // 2 :]])
    down_wide = widen(down_weight[0]).reshape(2, hid, width_pad)
    down_pieces = jnp.pad(down_wide, ((0, 0), (0, hid_pad - hid), (0, 0)))

    def by_layer(pieces):
        mine = jnp.where(core == 0, pieces[0], pieces[1])
        other = swap_cores(jnp.where(core == 0, pieces[1], pieces[0]))
        return [jnp.where(core == 0, mine, other), jnp.where(core == 0, other, mine)]

    def across_x(pieces):
        mine = jnp.where(x_index == 0, pieces[0], pieces[1])
        other = flip(jnp.where(x_index == 0, pieces[1], pieces[0]), *X_BIT)
        return jnp.stack([jnp.where(x_index == 0, mine, other), jnp.where(x_index == 0, other, mine)])

    qkv_l, up_l, out_l, down_l = by_layer(qkv_pieces), by_layer(up_pieces), by_layer(out_pieces), by_layer(down_pieces)

    order_zy = z_bits + y_bits
    order_yz = y_bits + z_bits
    layers = []
    token = None
    for l in range(2):
        start = (qkv_l[l], out_l[l], up_l[l], down_l[l])
        if token is not None:
            start = after(start, token)
        qkv_x = across_x(start[0])
        qkv_all, _ = gather_blocks(qkv_x, order_zy, places)
        out_all, _ = gather_blocks(start[1], [X_BIT] + order_zy, places_all)
        up_all, up_mid = gather_blocks(across_x(start[2]), order_zy, places)
        down_all, _ = gather_blocks(start[3], order_zy if l == 0 else order_yz, places)
        token = up_mid
        small_all = qkv_all.reshape(chips, part_pad, P_LANES)[:, part, :small_total]
        pieces, at = {}, 0
        for name in SMALL:
            pieces[name] = small_all[:, at : at + small_sizes[name]]
            at += small_sizes[name]

        def feature(name):
            return jnp.pad(pieces[name].astype(F32), ((0, 0), (0, part_pad - part))).reshape(1, width_pad)

        qv = pieces["b_qv"].astype(F32).reshape(2, H * HD)
        q_bias = lax.dynamic_slice_in_dim(qv[0], quarter * HSTEP * HD, HL * HD).reshape(HL, HD)
        v_bias = lax.dynamic_slice_in_dim(qv[1], quarter * HSTEP * HD, HL * HD)
        qkv_bias = jnp.concatenate(
            [
                jnp.concatenate([q_bias, jnp.zeros_like(q_bias)], axis=1).reshape(QK_LANES),
                v_bias,
                jnp.zeros((V_LANES - HL * HD,), F32),
            ]
        )[None]
        ups = pieces["up_bias"].astype(F32).reshape(all_groups, 2, 2, hid)
        up_mine = lax.dynamic_index_in_dim(
            lax.dynamic_index_in_dim(ups, x_index, 1, keepdims=False), core, 1, keepdims=False
        )
        up_bias_row = jnp.pad(up_mine, ((0, 0), (0, hid_pad - hid))).reshape(1, all_groups * hid_pad)
        out_both = in_core_order(out_all, swap_cores(out_all), 2)[:, :part].reshape(width, width_pad)
        out_mine = lax.dynamic_slice_in_dim(out_both, quarter * HSTEP * HD, HL * HD, axis=0)
        head_row = lax.broadcasted_iota(jnp.int32, (HL * HD, 1), 0) // HD
        own_head = (head_row > 0) | (quarter == 0)
        out_mine = pad_rows(jnp.where(own_head, out_mine, jnp.zeros_like(out_mine)), V_LANES)
        layers.append(
            {
                "qkv": qkv_all.reshape(width_pad, P_LANES),
                "qkv_bias": qkv_bias,
                "out": out_mine,
                "out_bias": feature("out_bias"),
                "up": up_all.reshape(width_pad, all_groups * hid_pad),
                "up_bias": up_bias_row,
                "down": down_all.reshape(all_groups * hid_pad, width_pad),
                "down_bias": feature("down_bias"),
                "gain_one": feature("gain_one"),
                "shift_one": feature("shift_one"),
                "gain_two": feature("gain_two"),
                "shift_two": feature("shift_two"),
            }
        )

    def sequence_of(group, turn):
        return group + groups * turn

    def to_groups(value):
        arrived = []
        for d in range(seq_count):
            target = (seq_index ^ d) >> 1
            send = []
            for turn in range(rounds):
                number = sequence_of(target, turn)
                taken = lax.dynamic_index_in_dim(value, jnp.minimum(number, micro - 1), 0, keepdims=False)
                send.append(jnp.where(number < micro, taken, jnp.zeros_like(taken)))
            send = jnp.stack(send)
            if d:
                pairs = [
                    (c * seq_count + s, c * seq_count + (s ^ d))
                    for c in range(2)
                    for s in range(seq_count)
                    if s // half_blocks == c
                ]
                send = lax.ppermute(send, ("section", "seq"), pairs)
            arrived.append(send)
        slots = []
        for i in range(half_blocks):
            offset = (core * half_blocks + i) ^ seq_index
            chosen = arrived[0]
            for d in range(1, seq_count):
                chosen = jnp.where(offset == d, arrived[d], chosen)
            slots.append(chosen)
        return jnp.concatenate(slots, axis=1)

    def to_blocks(value, layer):
        value = jnp.stack(value).reshape(rounds, half_blocks, block_rows, width)
        arrived = []
        for e in range(groups):
            wanted = (seq_index ^ (2 * e)) % half_blocks
            send = lax.dynamic_index_in_dim(value, wanted, 1, keepdims=False)
            pairs = [
                (c * seq_count + s, layer * seq_count + (s ^ (2 * e)))
                for c in range(2)
                for s in range(seq_count)
                if (s ^ (2 * e)) // half_blocks == c
            ]
            arrived.append(lax.ppermute(send, ("section", "seq"), pairs))
        result = []
        for number in range(micro):
            offset = (number % groups) ^ y_index
            turn = number // groups
            chosen = arrived[0][turn]
            for e in range(1, groups):
                chosen = jnp.where(offset == e, arrived[e][turn], chosen)
            result.append(chosen)
        return jnp.stack(result)

    positions = core * half_rows + jnp.arange(half_rows, dtype=jnp.int32)
    turn_lengths, live = [], []
    for turn in range(rounds):
        number = sequence_of(y_index, turn)
        at = dp_index * micro + jnp.minimum(number, micro - 1)
        turn_lengths.append(lax.dynamic_slice_in_dim(lengths, at, 1))
        live.append(number < micro)

    start_rows = widen(to_groups(inputs))
    grad_rows = widen(to_groups(cotangent))

    stored = [[None] * rounds for _ in range(2)]
    outputs = [[None] * rounds for _ in range(2)]
    rows_now = [start_rows[turn] for turn in range(rounds)]
    for l in range(2):
        for turn in range(rounds):
            result, kept = layer_forward(
                rows_now[turn].astype(F32), layers[l], turn_lengths[turn], mask, width
            )
            stored[l][turn] = (rows_now[turn],) + kept[1:]
            outputs[l][turn] = result.astype(BF16)
            rows_now[turn] = outputs[l][turn]

    acts_local = [to_blocks([narrow(o).astype(BF16) for o in outputs[l]], l) for l in range(2)]
    acts_local = jnp.where(core == 0, acts_local[0], acts_local[1])
    total_seqs = dealing.shape[0]
    numbers = jnp.arange(total_seqs, dtype=jnp.int32)
    position = jnp.sum(jnp.where(dealing[:, None] == numbers[None, :], numbers[:, None], 0), axis=0)
    target = lax.dynamic_slice_in_dim(position, dp_index * micro, micro) // micro
    anchor = lax.dynamic_slice_in_dim(dealing, dp_index * micro, micro) // micro
    dealt = []
    for d in range(dp_count):
        dest = dp_index ^ d
        send = acts_local[0]
        for i in range(1, micro):
            send = jnp.where(target[i] == dest, acts_local[i], send)
        if d:
            send = lax.ppermute(send, "dp", [(i, i ^ d) for i in range(dp_count)])
        dealt.append(send)
    acts = []
    for j in range(micro):
        offset = anchor[j] ^ dp_index
        chosen = dealt[0]
        for d in range(1, dp_count):
            chosen = jnp.where(offset == d, dealt[d], chosen)
        acts.append(chosen)
    acts = jnp.stack(acts)

    def total(values):
        return functools.reduce(jnp.add, values)

    def product(operands):
        return total([dot_0(a, b) for a, b in operands]).astype(BF16)

    once = (x_index == 0).astype(F32)
    grads = []
    for turn in range(rounds):
        valid = (positions < turn_lengths[turn]) & live[turn]
        grads.append(jnp.where(valid[:, None], grad_rows[turn].astype(F32), 0.0))

    finished = [None, None]
    sent_back = [None, None]
    for l in (1, 0):
        w = layers[l]
        smalls, operands = [], []
        middles = []
        for turn in range(rounds):
            grad_middle, small, ops = ffn_backward(grads[turn], stored[l][turn], w, mask, width)
            middles.append(grad_middle)
            smalls.append(small)
            operands.append(ops)
        d_down = product([ops["down"] for ops in operands])
        d_up = product([ops["up"] for ops in operands])
        down_done = scatter_blocks(d_down.reshape(all_groups, hid_pad, width_pad), list(reversed(order_zy)), places)
        up_done = scatter_blocks(
            d_up.reshape(all_groups, 2 * part_pad, all_groups * hid_pad), list(reversed(order_zy)), places
        )
        returned = []
        for turn in range(rounds):
            grad_in, small, ops = attn_layer_backward(
                middles[turn], stored[l][turn], w, turn_lengths[turn], mask, width
            )
            returned.append(grad_in.astype(BF16))
            smalls[turn].update(small)
            operands[turn].update(ops)
        sent_back[l] = returned
        if l == 1:
            grads = [r.astype(F32) for r in returned]
        d_out = product([ops["out"] for ops in operands])[: HL * HD]
        d_out = jnp.where(own_head, d_out, jnp.zeros_like(d_out))
        d_out_full = lax.dynamic_update_slice_in_dim(
            jnp.zeros((width, width_pad), BF16), d_out, quarter * HSTEP * HD, axis=0
        )
        d_out_full = jnp.pad(
            d_out_full.reshape(chips, part, 2, width_pad // 2), ((0, 0), (0, part_pad - part), (0, 0), (0, 0))
        )
        mine = jnp.where(core == 0, d_out_full[:, :, 0], d_out_full[:, :, 1])
        other = jnp.where(core == 0, d_out_full[:, :, 1], d_out_full[:, :, 0])
        d_out_half = (mine.astype(F32) + swap_cores(other).astype(F32)).astype(BF16)
        out_done = scatter_blocks(d_out_half, list(reversed([X_BIT] + order_zy)), places_all)

        sums = {name: total([small[name] for small in smalls]) for name in smalls[0]}

        def feature_sum(name):
            return sums[name].reshape(chips, part_pad)[:, :part] * once

        q_sum = sums["packed"][:QK_LANES].reshape(HL, 2, HD)[:, 0].reshape(HL * HD)
        v_sum = sums["packed"][QK_LANES : QK_LANES + HL * HD]
        qv_sum = jnp.stack(
            [
                lax.dynamic_update_slice_in_dim(
                    jnp.zeros((H * HD,), F32), jnp.where(own_head[:, 0], s, 0.0), quarter * HSTEP * HD, axis=0
                )
                for s in (q_sum, v_sum)
            ]
        ).reshape(chips, -1)
        up_sum = sums["up_bias"].reshape(all_groups, 1, 1, hid_pad)[..., :hid]
        at_x = jnp.arange(2)[None, :, None, None] == x_index
        at_c = jnp.arange(2)[None, None, :, None] == core
        up_sum = jnp.where(at_x & at_c, up_sum, 0.0).reshape(chips, -1)
        small_cols = jnp.concatenate(
            [qv_sum, feature_sum("out_bias"), up_sum]
            + [feature_sum(name) for name in ("down_bias", "gain_one", "shift_one", "gain_two", "shift_two")],
            axis=1,
        ).astype(BF16)
        small_cols = jnp.pad(small_cols, ((0, 0), (0, P_LANES - small_total)))[:, None, :]
        d_qkv = product([ops["qkv"] for ops in operands]).reshape(chips, part_pad, P_LANES)
        at_row = lax.broadcasted_iota(jnp.int32, (1, part_pad, 1), 1) == part
        d_qkv = jnp.where(at_row, small_cols, d_qkv)
        qkv_done = scatter_blocks(
            d_qkv.reshape(all_groups, 2 * part_pad, P_LANES), list(reversed(order_zy)), places
        )
        finished[l] = (qkv_done, out_done, up_done, down_done)

    def back_across_x(value):
        low, high = value[:part_pad], value[part_pad:]
        mine = jnp.where(x_index == 0, low, high)
        other = flip(jnp.where(x_index == 0, high, low), *X_BIT)
        return jnp.stack([jnp.where(x_index == 0, mine, other), jnp.where(x_index == 0, other, mine)])

    def own_layer(first, second):
        mine = jnp.where(core == 0, first, second)
        other = swap_cores(jnp.where(core == 0, second, first))
        return [jnp.where(core == 0, mine, other), jnp.where(core == 0, other, mine)]

    qkv_c = own_layer(*[back_across_x(finished[l][0]) for l in range(2)])
    up_c = own_layer(*[back_across_x(finished[l][2]) for l in range(2)])
    out_c = own_layer(finished[0][1], finished[1][1])
    down_c = own_layer(finished[0][3], finished[1][3])

    def heads_sum(lanes_of):
        parts = []
        for x in range(2):
            for c in range(2):
                q = 2 * x + c
                piece = lanes_of(qkv_c[c][x, :part].astype(F32))
                own = jnp.arange(HL * HD) >= (0 if q == 0 else HD)
                piece = jnp.where(own[None], piece, 0.0)
                parts.append(jnp.pad(piece, ((0, 0), (HSTEP * q * HD, (H - HL - HSTEP * q) * HD))))
        return total(parts)

    def qk_half(which):
        return lambda piece: piece[:, :QK_LANES].reshape(part, HL, 2, HD)[:, :, which].reshape(part, HL * HD)

    grad_w_qkv = jnp.concatenate(
        [heads_sum(qk_half(0)), heads_sum(qk_half(1)), heads_sum(lambda p: p[:, QK_LANES : QK_LANES + HL * HD])],
        axis=1,
    )
    grad_w_out = narrow(jnp.concatenate([out_c[0][:part], out_c[1][:part]], axis=1))
    up_parts = jnp.stack(
        [
            jnp.stack(
                [up_c[c][x, :part].reshape(part, all_groups, hid_pad)[..., :hid] for c in range(2)], axis=2
            )
            for x in range(2)
        ],
        axis=2,
    )
    grad_w_up = up_parts.astype(F32).reshape(part, -1)
    grad_w_down = narrow(jnp.concatenate([down_c[0][:hid], down_c[1][:hid]], axis=0))
    small_sum = total([qkv_c[c][x, part, :small_total].astype(F32) for x in range(2) for c in range(2)])
    small_out, at = {}, 0
    for name in SMALL:
        small_out[name] = small_sum[at : at + small_sizes[name]]
        at += small_sizes[name]

    grads_local = [to_blocks([narrow(r).astype(BF16) for r in sent_back[l]], l) for l in range(2)]
    input_grad = jnp.where(core == 0, grads_local[0], grads_local[1])
    return (
        acts[None],
        input_grad[None],
        grad_w_qkv[None],
        small_out["b_qv"][None],
        grad_w_out[None],
        small_out["out_bias"][None],
        grad_w_up[None],
        small_out["up_bias"][None],
        grad_w_down[None],
        small_out["down_bias"][None],
        small_out["gain_one"][None],
        small_out["shift_one"][None],
        small_out["gain_two"][None],
        small_out["shift_two"][None],
    )


def solution(mesh):
    wide = P("section", ("dp", "seq"), None)
    thin = P("section", ("dp", "seq"))
    in_specs = (
        P("dp", "seq", None),
        P("dp", "seq", None),
        P(),
        P(),
        wide,
        thin,
        wide,
        thin,
        wide,
        thin,
        wide,
        thin,
        thin,
        thin,
        thin,
        thin,
    )
    out_specs = (
        P("section", "dp", "seq", None),
        P("section", "dp", "seq", None),
        wide,
        thin,
        wide,
        thin,
        wide,
        thin,
        wide,
        thin,
        thin,
        thin,
        thin,
        thin,
    )
    return jax.shard_map(per_device, mesh=mesh, in_specs=in_specs, out_specs=out_specs, check_vma=False)
```

```python
import functools

import jax
import jax.numpy as jnp
from jax import lax
from jax.experimental import pallas as pl
from jax.experimental.pallas import tpu as pltpu
from jax.sharding import PartitionSpec as P

H = 25
HD = 64
QUARTERS = 4
HL = -(-H // QUARTERS)
HSTEP = (H - HL) // (QUARTERS - 1)
PAIRS = -(-HL // 2)
V_LANES = PAIRS * 2 * HD
P_LANES = 3 * V_LANES
ROW_BLOCK = 256
F32 = jnp.float32
BF16 = jnp.bfloat16


def round_up(value, by):
    return -(-value // by) * by


def lane_map_kernel(places, x_ref, o_ref):
    width, wide = x_ref.shape[1], o_ref.shape[1]
    for at in range(0, wide, 128):
        end = min(at + 128, wide)
        column = at + lax.broadcasted_iota(jnp.int32, (128, end - at), 1)
        source = places.of(column)
        total = None
        for low in sorted({p // 128 * 128 for p in (places(j) for j in range(at, end)) if p >= 0}):
            high = min(low + 128, width)
            row = low + lax.broadcasted_iota(jnp.int32, (high - low, end - at), 0)
            chosen = (row == source[: high - low]).astype(BF16)
            term = jnp.dot(x_ref[:, low:high], chosen, preferred_element_type=F32)
            total = term if total is None else total + term
        o_ref[:, at:end] = total.astype(o_ref.dtype)


class Spread:
    def __init__(self, part, part_pad):
        self.part, self.part_pad = part, part_pad

    def __call__(self, j):
        return j // self.part_pad * self.part + j % self.part_pad if j % self.part_pad < self.part else -1

    def of(self, j):
        inside = lax.rem(j, self.part_pad)
        return jnp.where(inside < self.part, lax.div(j, self.part_pad) * self.part + inside, -1)


class Gather:
    def __init__(self, part, part_pad):
        self.part, self.part_pad = part, part_pad

    def __call__(self, j):
        return j // self.part * self.part_pad + j % self.part

    def of(self, j):
        return lax.div(j, self.part) * self.part_pad + lax.rem(j, self.part)


def lane_map(value, places, wide, dtype=BF16):
    shape = value.shape[:-1] + (wide,)
    flat = value.reshape(-1, value.shape[-1])
    rows = flat.shape[0]
    block = rows if rows % 256 else 256
    result = pl.pallas_call(
        functools.partial(lane_map_kernel, places),
        grid=(rows // block,),
        in_specs=[pl.BlockSpec((block, flat.shape[1]), lambda i: (i, 0))],
        out_specs=pl.BlockSpec((block, wide), lambda i: (i, 0)),
        out_shape=jax.ShapeDtypeStruct((rows, wide), dtype),
        compiler_params=pltpu.CompilerParams(vmem_limit_bytes=32 * 2**20),
        cost_estimate=FREE,
        name="lane_map",
    )(flat)
    return result.reshape(shape)


NT = (((1,), (1,)), ((), ()))
TN = (((0,), (0,)), ((), ()))
FREE = pl.CostEstimate(flops=0, bytes_accessed=0, transcendentals=0)


def on_each_part(info_ref, parts, body):
    if parts == 1:
        body(0)
        return
    for part in range(parts):
        pl.when(info_ref[info_ref.shape[0] - 1] == part)(functools.partial(body, part))


def heads_of_pair(body):
    if HL % 2 == 0:
        body((0, 1))
        return
    last = pl.program_id(1) == PAIRS - 1
    pl.when(jnp.logical_not(last))(functools.partial(body, (0, 1)))
    pl.when(last)(functools.partial(body, (0,)))


def attn_fwd_kernel(info_ref, q_ref, k_ref, v_ref, o_ref, lse_ref):
    total, rows = k_ref.shape[0], o_ref.shape[0]
    length = info_ref[pl.program_id(0)]
    block = min(ROW_BLOCK, rows)
    lower = lax.broadcasted_iota(jnp.int32, (block, 2 * HD), 1) < HD
    keep = jnp.where(lax.broadcasted_iota(jnp.int32, (total, 1), 0) < length, 0.0, -1e30)

    def body(heads, half):
        for i in range(rows // block):
            first = half * rows + i * block
            end = first + block
            key = lax.broadcasted_iota(jnp.int32, (end, block), 0)
            query = lax.broadcasted_iota(jnp.int32, (end, block), 1) + first
            probs = []
            for a in heads:
                mine = lower if a == 0 else jnp.logical_not(lower)
                q = jnp.where(mine, q_ref[first:end, :] * jnp.asarray(HD**-0.5, BF16), jnp.zeros((), BF16))
                scores = lax.dot_general(k_ref[:end, :], q, NT, preferred_element_type=F32) + keep[:end]
                scores = jnp.where(key <= query, scores, -1e30)
                top = jnp.max(scores, axis=0, keepdims=True)
                weights = jnp.exp(scores - top)
                below = jnp.sum(weights, axis=0, keepdims=True)
                lse_ref[a : a + 1, i * block : (i + 1) * block] = top + jnp.log(below)
                probs.append((weights * (1.0 / below)).astype(BF16))
            parts = [lax.dot_general(p, v_ref[:end, :], TN, preferred_element_type=F32) for p in probs]
            upper = parts[1] if len(heads) == 2 else jnp.zeros_like(parts[0])
            o_ref[i * block : (i + 1) * block, :] = jnp.where(lower, parts[0], upper).astype(BF16)

    lse_ref[...] = jnp.zeros_like(lse_ref)
    heads_of_pair(lambda heads: on_each_part(info_ref, total // rows, functools.partial(body, heads)))


def pair_spec(rows, lanes, offset=0):
    return pl.BlockSpec((None, rows, lanes), lambda i, j: (i, 0, j + offset))


def stats_spec(rows):
    return pl.BlockSpec((None, None, 2, rows), lambda i, j: (i, j, 0, 0))


def attn_forward(packed, info, rows):
    count, total, _ = packed.shape
    return pl.pallas_call(
        attn_fwd_kernel,
        grid=(count, PAIRS),
        in_specs=[
            pl.BlockSpec(memory_space=pltpu.SMEM),
            pair_spec(total, 2 * HD),
            pair_spec(total, 2 * HD, PAIRS),
            pair_spec(total, 2 * HD, 2 * PAIRS),
        ],
        out_specs=[pair_spec(rows, 2 * HD), stats_spec(rows)],
        out_shape=[
            jax.ShapeDtypeStruct((count, rows, V_LANES), BF16),
            jax.ShapeDtypeStruct((count, PAIRS, 2, rows), F32),
        ],
        compiler_params=pltpu.CompilerParams(vmem_limit_bytes=48 * 2**20),
        cost_estimate=FREE,
        name="attn_fwd",
    )(info, packed, packed, packed)


def attn_bwd_kernel(info_ref, q_ref, k_ref, v_ref, g_ref, o_ref, lse_ref, out_ref):
    total, rows = k_ref.shape[0], g_ref.shape[0]
    block = min(2 * ROW_BLOCK, rows)
    count = total // block
    pair = pl.program_id(1)
    length = info_ref[pl.program_id(0)]
    lane = lax.broadcasted_iota(jnp.int32, (block, 2 * HD), 1)
    key = lax.broadcasted_iota(jnp.int32, (block, block), 0)
    query = lax.broadcasted_iota(jnp.int32, (block, block), 1)
    key_row = lax.broadcasted_iota(jnp.int32, (block, 1), 0)

    def body(heads, half):
        nothing = jnp.zeros((block, 2 * HD), F32)
        dq, dk, dv = {}, {}, {}
        for i in range(rows // block):
            at = slice(i * block, (i + 1) * block)
            place = half * rows // block + i
            g = g_ref[at, :]
            product = g.astype(F32) * o_ref[at, :].astype(F32)
            mine = {}
            for a in heads:
                lanes = (lane < HD) if a == 0 else (lane >= HD)
                inner = lax.dot_general(
                    jnp.ones((8, 2 * HD), F32),
                    jnp.where(lanes, product, 0.0),
                    NT,
                    preferred_element_type=F32,
                    precision=lax.Precision.HIGHEST,
                )[0:1]
                q = q_ref[place * block : (place + 1) * block, :] * jnp.asarray(HD**-0.5, BF16)
                q = jnp.where(lanes, q, jnp.zeros_like(q))
                mine[a] = (q, jnp.where(lanes, g, jnp.zeros_like(g)), inner, lse_ref[a : a + 1, at])
            for j in range(place + 1):
                keys = slice(j * block, (j + 1) * block)
                keep = jnp.where(key_row < length - j * block, 0.0, -1e30)
                for a in heads:
                    q, g_mine, inner, lse = mine[a]
                    k = k_ref[keys, :]
                    scores = lax.dot_general(k, q, NT, preferred_element_type=F32) + keep
                    if j == place:
                        scores = jnp.where(key <= query, scores, -1e30)
                    probs = jnp.exp(scores - lse)
                    gprobs = lax.dot_general(v_ref[keys, :], g_mine, NT, preferred_element_type=F32)
                    gscores = (probs * (gprobs - inner)).astype(BF16)
                    dq[a, place] = dq.get((a, place), 0.0) + lax.dot_general(
                        gscores, k, TN, preferred_element_type=F32
                    )
                    dk[a, j] = dk.get((a, j), 0.0) + jnp.dot(gscores, q, preferred_element_type=F32)
                    dv[j] = dv.get(j, 0.0) + jnp.dot(probs.astype(BF16), g_mine, preferred_element_type=F32)
        for j in range(count):
            at = slice(j * block, (j + 1) * block)
            low, high = heads[0], heads[-1]
            dq_both = jnp.where(lane < HD, dq.get((low, j), nothing), dq.get((high, j), nothing)) * HD**-0.5
            dk_both = jnp.where(lane < HD, dk.get((low, j), nothing), dk.get((high, j), nothing))
            for which, value in enumerate((dq_both, dk_both, dv.get(j, nothing))):
                start = pl.multiple_of(which * V_LANES + pair * 2 * HD, 2 * HD)
                out_ref[at, pl.ds(start, 2 * HD)] = value.astype(BF16)

    heads_of_pair(lambda heads: on_each_part(info_ref, total // rows, functools.partial(body, heads)))


def attn_backward(packed, grad, attended, lse, info):
    (count, total, _), rows = packed.shape, grad.shape[1]
    return pl.pallas_call(
        attn_bwd_kernel,
        grid=(count, PAIRS),
        in_specs=[
            pl.BlockSpec(memory_space=pltpu.SMEM),
            pair_spec(total, 2 * HD),
            pair_spec(total, 2 * HD, PAIRS),
            pair_spec(total, 2 * HD, 2 * PAIRS),
            pair_spec(rows, 2 * HD),
            pair_spec(rows, 2 * HD),
            stats_spec(rows),
        ],
        out_specs=pl.BlockSpec((None, total, P_LANES), lambda i, j: (i, 0, 0)),
        out_shape=jax.ShapeDtypeStruct((count, total, P_LANES), BF16),
        compiler_params=pltpu.CompilerParams(vmem_limit_bytes=56 * 2**20),
        cost_estimate=FREE,
        name="attn_bwd",
    )(info, packed, packed, packed, grad, attended, lse)


PAIR = "x"


def flip(value, axis):
    return lax.ppermute(value, axis, [(0, 1), (1, 0)])


def in_turn(mine, other, mine_at, axis):
    shape = [1] * mine.ndim
    shape[axis] = 2
    place = lax.broadcasted_iota(jnp.int32, tuple(shape), axis)
    return jnp.where(place == mine_at, mine, other)


def pick(value, at, axis=0):
    return lax.dynamic_slice_in_dim(value, at, 1, axis=axis)


def there(*tokens):
    result = None
    for leaf in jax.tree.leaves(tokens):
        first = lax.slice(leaf, (0,) * leaf.ndim, (1,) * leaf.ndim).reshape(())
        result = (first == first) if result is None else result & (first == first)
    return result


def tied(value, *tokens):
    if not jax.tree.leaves(tokens):
        return value
    return value + jnp.where(there(tokens), 0, 1).astype(value.dtype)


def rows_of_both(own):
    count, rows, width = own.shape
    both = in_turn(own[:, None], flip(own, "section")[:, None], lax.axis_index("section"), 1)
    return both.reshape(count, 2 * rows, width)


def chip_rows(partial):
    count, rows, width = partial.shape
    core = lax.axis_index("section")
    split = partial.reshape(count, 2, rows // 2, width)
    other = flip(pick(split, 1 - core, 1)[:, 0], "section")
    return (pick(split, core, 1)[:, 0].astype(F32) + other.astype(F32)).astype(BF16)


class PairSum:
    def __init__(self):
        self.before = ()

    def hold(self, value):
        self.before += (value,)

    def __call__(self, chip):
        arrived = flip(tied(chip, self.before), PAIR)
        self.before = (arrived,)
        return chip.astype(F32) + arrived.astype(F32)


def dot(a, b):
    flat = jnp.dot(a.reshape(-1, a.shape[-1]), b, preferred_element_type=F32)
    return flat.reshape(a.shape[:-1] + (b.shape[1],))


def dot_t(a, b):
    flat = lax.dot_general(a.reshape(-1, a.shape[-1]), b, NT, preferred_element_type=F32)
    return flat.reshape(a.shape[:-1] + (b.shape[0],))


def dot_0(a, b):
    return lax.dot_general(a.reshape(-1, a.shape[-1]), b.reshape(-1, b.shape[-1]), TN, preferred_element_type=F32)


def row_sum(value):
    return jnp.sum(value.astype(F32), axis=(0, 1))


def gelu_parts(u):
    t = jnp.tanh(0.7978845608 * (u + 0.044715 * u * u * u))
    return t


def gelu(u):
    return 0.5 * u * (1.0 + gelu_parts(u))


def gelu_slope(u):
    t = gelu_parts(u)
    return 0.5 * (1.0 + t) + 0.5 * u * (1.0 - t * t) * 0.7978845608 * (1.0 + 3 * 0.044715 * u * u)


def norm_stats(rows, mask, width):
    average = jnp.sum(rows, axis=-1, keepdims=True) / width
    centered = (rows - average) * mask
    variance = jnp.sum(centered * centered, axis=-1, keepdims=True) / width
    scale = lax.rsqrt(variance + 1e-05)
    return centered * scale, scale


def norm_back(grad, rows, gain, mask, width):
    hat, scale = norm_stats(rows, mask, width)
    inner = grad * gain
    mean_one = jnp.sum(inner, axis=-1, keepdims=True) / width
    mean_two = jnp.sum(inner * hat, axis=-1, keepdims=True) / width
    back = scale * (inner - mean_one - hat * mean_two) * mask
    return back, row_sum(grad * hat), row_sum(grad * mask)


def whole_sequence(packed):
    parts = lax.axis_size("y")
    if parts == 2:
        other = lax.ppermute(packed[..., V_LANES:], "y", [(0, 1)])
        other = jnp.pad(other, ((0, 0), (0, 0), (V_LANES, 0)))
        both = in_turn(packed[:, None], other[:, None], lax.axis_index("y"), 1)
    else:
        both = lax.all_gather(packed, "y", axis=1)
    return both.reshape(packed.shape[0], parts * packed.shape[1], packed.shape[2])


def own_rows(grad):
    parts = lax.axis_size("y")
    rows = grad.shape[1] // parts
    if parts != 2:
        return lax.psum_scatter(grad, "y", scatter_dimension=1, tiled=True)
    other = lax.ppermute(grad[:, :rows, V_LANES:], "y", [(1, 0)])
    other = jnp.pad(other, ((0, 0), (0, 0), (V_LANES, 0)))
    own = lax.dynamic_slice_in_dim(grad, lax.axis_index("y") * rows, rows, axis=1)
    return (own.astype(F32) + other.astype(F32)).astype(BF16)


def project_stage(rows, w, mask, width):
    hat, _ = norm_stats(rows.astype(F32), mask, width)
    normed = rows_of_both((hat * w["gain_one"] + w["shift_one"]).astype(BF16))
    packed = (dot(normed, w["qkv"]) + w["qkv_bias"]).astype(BF16)
    return normed, whole_sequence(packed)


def attend_stage(normed, packed, w, info):
    attended, lse = attn_forward(packed, info, normed.shape[1])
    return dot(attended, w["out"]).astype(BF16), (normed, packed, attended, lse)


def ffn_stage(middle, w, mask, width):
    hat, _ = norm_stats(middle, mask, width)
    normed = rows_of_both((hat * w["gain_two"] + w["shift_two"]).astype(BF16))
    upward = dot(normed, w["up"]) + w["up_bias"]
    hidden = gelu(upward).astype(BF16)
    partial = dot(hidden, w["down"]).astype(BF16)
    return partial, (normed, upward.astype(BF16), hidden)


def ffn_back_stage(grad_out, kept, w, token=()):
    normed, upward, hidden = kept
    grad_down = tied(grad_out.astype(BF16), token)
    b_down = row_sum(grad_down)
    grad_down = rows_of_both(grad_down)
    grad_up = (dot_t(grad_down, w["down"]) * gelu_slope(upward.astype(F32))).astype(BF16)
    b_up = row_sum(grad_up)
    partial = dot_t(grad_up, w["up"]).astype(BF16)
    return partial, {"down_bias": b_down, "up_bias": b_up}, {"down": (hidden, grad_down), "up": (normed, grad_up)}


def branch_stage(grad_middle, kept, token=()):
    grad_branch = tied(grad_middle.astype(BF16), token)
    return rows_of_both(grad_branch), {"out_bias": row_sum(grad_branch)}


def attend_back_stage(grad_branch, kept, w, info):
    normed, packed, attended, lse = kept
    grad_attended = dot_t(grad_branch, w["out"]).astype(BF16)
    return attn_backward(packed, grad_attended, attended, lse, info)


def project_back_stage(grad_packed, kept, w):
    grad_packed = own_rows(grad_packed)
    b_packed = row_sum(grad_packed)
    partial = dot_t(grad_packed, w["qkv"]).astype(BF16)
    return partial, {"packed": b_packed}, {"qkv": (kept[0], grad_packed)}


SMALL = ("b_qv", "out_bias", "up_bias", "down_bias", "gain_one", "shift_one", "gain_two", "shift_two")


def per_device(
    inputs,
    cotangent,
    lengths,
    dealing,
    query_key_value_weight,
    b_qv,
    attention_out_weight,
    attention_out_bias,
    up_weight,
    up_bias,
    down_weight,
    down_bias,
    gain_one,
    shift_one,
    gain_two,
    shift_two,
):
    micro, block_rows, width = inputs.shape
    dp_count, y_count = lax.axis_size("dp"), lax.axis_size("y")
    chips = 2 * dp_count * y_count
    all_groups = dp_count * y_count
    core, dp_index = lax.axis_index("section"), lax.axis_index("dp")
    x_index, y_index = lax.axis_index("x"), lax.axis_index("y")
    quarter = 2 * x_index + core
    part = query_key_value_weight.shape[1]
    part_pad = round_up(part + 1, 8)
    width_pad = chips * part_pad
    hid = down_weight.shape[1] // 2
    hid_pad = round_up(hid, 8)
    while all_groups * hid_pad % 128:
        hid_pad += 8

    lane = lax.broadcasted_iota(jnp.int32, (1, width_pad), 1)
    mask = (lane % part_pad < part).astype(F32)
    local = lax.broadcasted_iota(jnp.int32, (V_LANES, width_pad), 0)
    column = lax.broadcasted_iota(jnp.int32, (V_LANES, width_pad), 1)
    whole_row = local + quarter * HSTEP * HD
    own_local = (local < HL * HD) & ((local >= HD) | (quarter == 0))
    placed = ((column == whole_row // part * part_pad + whole_row % part) & own_local).astype(BF16)
    side = round_up(width_pad // 2, 128)
    far = width_pad - side

    def widen(value):
        return lane_map(value, Spread(part, part_pad), width_pad)

    def narrow(value, dtype=BF16):
        return lane_map(value.astype(BF16), Gather(part, part_pad), width, dtype)

    def pad_rows(value, rows):
        return jnp.pad(value, ((0, rows - value.shape[0]), (0, 0)))

    small_in = dict(
        zip(SMALL, (b_qv, attention_out_bias, up_bias, down_bias, gain_one, shift_one, gain_two, shift_two))
    )
    small_sizes = {name: value.shape[1] for name, value in small_in.items()}
    small_row = jnp.concatenate([small_in[name][0] for name in SMALL])
    small_total = small_row.shape[0]

    shard = query_key_value_weight[0].reshape(part, 3, H, HD)

    out_wide = pad_rows(widen(attention_out_weight[0]), part_pad)
    out_pieces = jnp.stack([jnp.stack([out_wide[:, at : at + side]] * 2) for at in (0, far)])

    def attn_piece(q):
        from_head = HSTEP * q
        heads = shard[:, :, from_head : from_head + HL]
        body = jnp.pad(heads.reshape(part, 3, HL * HD), ((0, 0), (0, 0), (0, V_LANES - HL * HD)))
        body = body.reshape(part, P_LANES)
        row = jnp.pad(small_row, (0, P_LANES - small_total))[None]
        return pad_rows(jnp.concatenate([body, row], axis=0), part_pad)

    up_shard = up_weight[0].reshape(part, all_groups, 2, 2, hid)

    def up_piece(q):
        body = up_shard[:, :, q // 2, q % 2]
        body = jnp.pad(body, ((0, 0), (0, 0), (0, hid_pad - hid))).reshape(part, all_groups * hid_pad)
        return pad_rows(body, part_pad)

    attn_pieces = jnp.stack([jnp.stack([attn_piece(2 * x + c) for x in range(2)]) for c in range(2)])
    up_pieces = jnp.stack([jnp.stack([up_piece(2 * x + c) for x in range(2)]) for c in range(2)])
    down_wide = widen(down_weight[0]).reshape(2, hid, width_pad)
    down_pieces = jnp.pad(down_wide, ((0, 0), (0, hid_pad - hid), (0, 0)))

    def by_layer(pieces):
        mine, other = pick(pieces, core)[0], flip(pick(pieces, 1 - core)[0], "section")
        return [jnp.where(core == 0, mine, other), jnp.where(core == 0, other, mine)]

    def across_pair(pieces):
        both = in_turn(pick(pieces, x_index), flip(pick(pieces, 1 - x_index), PAIR), x_index, 0)
        return both.reshape(2 * part_pad, both.shape[-1])

    groups = ("dp", "y")
    down_l = by_layer(down_pieces)
    attn_l = [across_pair(pieces) for pieces in by_layer(jnp.concatenate([attn_pieces, out_pieces], axis=-1))]
    up_l = [across_pair(pieces) for pieces in by_layer(up_pieces)]
    def gather(piece, *tokens):
        return lax.all_gather(tied(piece, tokens), groups, axis=0)

    down_first, attn_first = gather(down_l[0]), gather(attn_l[0])
    up_first = gather(up_l[0], down_first)
    weights = []

    def layer_of(attn_all, up_all, down_all):
        if attn_all is None:
            return {"down": down_all.reshape(all_groups * hid_pad, width_pad)}
        attn_all = attn_all.reshape(width_pad, P_LANES + side)
        qkv_all, out_all = attn_all[:, :P_LANES], attn_all[:, P_LANES:]
        small_all = qkv_all.reshape(chips, part_pad, P_LANES)[:, part, :small_total]
        pieces, at = {}, 0
        for name in SMALL:
            pieces[name] = small_all[:, at : at + small_sizes[name]]
            at += small_sizes[name]

        def feature(name):
            return jnp.pad(pieces[name].astype(F32), ((0, 0), (0, part_pad - part))).reshape(1, width_pad)

        qv = pieces["b_qv"].astype(F32).reshape(2, H * HD)
        own_qv = lax.dynamic_slice_in_dim(qv, quarter * HSTEP * HD, HL * HD, axis=1)
        own_qv = jnp.pad(own_qv, ((0, 0), (0, V_LANES - HL * HD)))
        qkv_bias = jnp.concatenate([own_qv[0], jnp.zeros((V_LANES,), F32), own_qv[1]])[None]
        ups = pieces["up_bias"].astype(F32).reshape(all_groups, 2, 2, hid)
        up_mine = lax.dynamic_index_in_dim(
            lax.dynamic_index_in_dim(ups, x_index, 1, keepdims=False), core, 1, keepdims=False
        )
        up_bias_row = jnp.pad(up_mine, ((0, 0), (0, hid_pad - hid))).reshape(1, all_groups * hid_pad)
        sides = in_turn(out_all[None], flip(out_all, "section")[None], core, 0)
        out_both = jnp.concatenate([sides[0], sides[1, :, side - far :]], axis=1)
        out_mine = dot(placed, out_both).astype(BF16)
        return {
                "qkv": qkv_all.reshape(width_pad, P_LANES),
                "qkv_bias": qkv_bias,
                "out": out_mine,
                "out_bias": feature("out_bias"),
                "up": up_all.reshape(width_pad, all_groups * hid_pad),
                "up_bias": up_bias_row,
                "down": None if down_all is None else down_all.reshape(all_groups * hid_pad, width_pad),
                "down_bias": feature("down_bias"),
                "gain_one": feature("gain_one"),
                "shift_one": feature("shift_one"),
                "gain_two": feature("gain_two"),
                "shift_two": feature("shift_two"),
        }

    rounds = [range(0, micro - micro // 2), range(micro - micro // 2, micro)]
    turns = range(len(rounds))
    CORE_X = ("section", "x")

    def to_rounds(value):
        rows = jnp.where(core == x_index, value, lax.ppermute(value, CORE_X, [(0, 1), (3, 2)]))
        rows = widen(rows)
        return [rows[r.start : r.stop] for r in rounds]

    def to_blocks(value, layer):
        rows = narrow(jnp.concatenate(value, axis=0))
        pairs = [(0, 2 * layer), (3, 2 * layer + 1), (1, 2 - 2 * layer), (2, 3 - 2 * layer)]
        return lax.ppermute(rows, CORE_X, pairs)

    own_lengths = lax.dynamic_slice_in_dim(lengths, dp_index * micro, micro)
    positions = (2 * y_index + core) * block_rows + jnp.arange(block_rows, dtype=jnp.int32)
    turn_info = [jnp.concatenate([own_lengths[r.start : r.stop], y_index[None].astype(jnp.int32)]) for r in rounds]

    start_rows = to_rounds(inputs)
    grad_rows = to_rounds(tied(cotangent, up_first))

    kept_attn = [[None] * len(rounds) for _ in range(2)]
    kept_ffn = [[None] * len(rounds) for _ in range(2)]
    middles = [[None] * len(rounds) for _ in range(2)]
    entering = [start_rows, None]
    pair_sum = PairSum()
    outputs = [None, None]
    layers = [layer_of(attn_first, up_first, down_first), None]
    for l in range(2):
        w = layers[l]
        partials, chip = [None] * len(rounds), [None] * len(rounds)
        projected = [None] * len(rounds)
        for turn in reversed(turns):
            projected[turn] = project_stage(entering[l][turn], w, mask, width)
        if l == 0:
            attn_second = gather(attn_l[1], projected[0][1], up_first)
        else:
            weights.append(gather(down_l[1], projected[0][1]))
            layers[1].update(layer_of(None, None, weights[-1]))
        for turn in turns:
            partials[turn], kept_attn[l][turn] = attend_stage(*projected[turn], w, turn_info[turn])
        for turn in turns:
            middles[l][turn] = entering[l][turn].astype(F32) + pair_sum(chip_rows(partials[turn])) + w["out_bias"]
            partials[turn], kept_ffn[l][turn] = ffn_stage(middles[l][turn], w, mask, width)
            if l == 0 and turn == 0:
                up_second = gather(up_l[1], partials[turn])
                layers[1] = layer_of(attn_second, up_second, None)
        outputs[l] = [
            (middles[l][turn] + pair_sum(chip_rows(partials[turn])) + w["down_bias"]).astype(BF16) for turn in turns
        ]
        if l == 0:
            entering[1] = outputs[0]

    def deal(token):
        acts_local = [to_blocks(outputs[l], l) for l in range(2)]
        acts_local = jnp.where(core == 0, acts_local[0], acts_local[1])
        total_seqs = dealing.shape[0]
        numbers = jnp.arange(total_seqs, dtype=jnp.int32)
        position = jnp.sum(jnp.where(dealing[:, None] == numbers[None, :], numbers[:, None], 0), axis=0)
        target = lax.dynamic_slice_in_dim(position, dp_index * micro, micro) // micro
        anchor = lax.dynamic_slice_in_dim(dealing, dp_index * micro, micro) // micro
        dealt = []
        for d in range(dp_count):
            dest = dp_index ^ d
            send = acts_local[0]
            for i in range(1, micro):
                send = jnp.where(target[i] == dest, acts_local[i], send)
            send = tied(send, token)
            if d:
                send = lax.ppermute(send, "dp", [(i, i ^ d) for i in range(dp_count)])
            dealt.append(send)
        result = []
        for j in range(micro):
            offset = anchor[j] ^ dp_index
            chosen = dealt[0]
            for d in range(1, dp_count):
                chosen = jnp.where(offset == d, dealt[d], chosen)
            result.append(chosen)
        return jnp.stack(result)

    def total(values):
        return functools.reduce(jnp.add, values)

    def product(operands):
        return total([dot_0(a, b) for a, b in operands]).astype(BF16)

    once = (x_index == 0).astype(F32)
    valid = [positions[None] < own_lengths[r.start : r.stop, None] for r in rounds]
    grads = [jnp.where(valid[turn][..., None], grad_rows[turn].astype(F32), 0.0) for turn in turns]

    def scattered(value, rows):
        value = value.reshape(all_groups, rows, value.shape[-1])
        return lax.psum_scatter(value, groups, scatter_dimension=0, tiled=False)

    finished = [None, None]
    token = ()
    sent_back = [None, None]
    for l in (1, 0):
        w = layers[l]
        smalls, operands, partials = [{} for _ in turns], [{} for _ in turns], [None] * len(rounds)
        for turn in turns:
            partials[turn], small, ops = ffn_back_stage(grads[turn], kept_ffn[l][turn], w, token)
            smalls[turn].update(small)
            operands[turn].update(ops)
        d_down = product([ops["down"] for ops in operands])
        d_up = product([ops["up"] for ops in operands])
        token = (d_down, d_up)
        down_done = scattered(d_down, hid_pad)
        up_done = scattered(d_up, 2 * part_pad)
        grad_middles = [None] * len(rounds)
        for turn in turns:
            if l == 0 and turn == 1:
                pair_sum.hold(finished[1]["up"])
            back, gain, shift = norm_back(
                pair_sum(chip_rows(partials[turn])), middles[l][turn], w["gain_two"], mask, width
            )
            smalls[turn].update({"gain_two": gain, "shift_two": shift})
            grad_middles[turn] = grads[turn] + back
        branches = [None] * len(rounds)
        for turn in turns:
            branches[turn], small = branch_stage(grad_middles[turn], kept_attn[l][turn], token)
            smalls[turn].update(small)
            operands[turn]["out"] = (kept_attn[l][turn][2], branches[turn])
        if l == 0:
            acts = deal(tuple(branches))
        d_out = dot_0(placed, product([ops["out"] for ops in operands])).astype(BF16)
        out_own = lax.dynamic_slice_in_dim(d_out, core * far, side, axis=1)
        out_other = flip(lax.dynamic_slice_in_dim(d_out, (1 - core) * far, side, axis=1), "section")
        d_out = (out_own.astype(F32) + out_other.astype(F32)).astype(BF16)
        out_done = scattered(d_out, 2 * part_pad)
        grad_packed, before = [None] * len(rounds), ()
        for turn in reversed(turns):
            grad_packed[turn] = attend_back_stage(
                branches[turn], kept_attn[l][turn], w, turn_info[turn] + jnp.where(there(before), 0, 1)
                if before
                else turn_info[turn]
            )
            before = (grad_packed[turn],)
        for turn in turns:
            partials[turn], small, ops = project_back_stage(grad_packed[turn], kept_attn[l][turn], w)
            smalls[turn].update(small)
            operands[turn].update(ops)
        d_qkv = product([ops["qkv"] for ops in operands])
        token = (d_qkv, out_done)
        returned = []
        for turn in turns:
            if l == 1 and turn == 1:
                pair_sum.hold(down_done)
            if l == 0 and turn == 1:
                pair_sum.hold((acts, finished[1]["qkv"]))
            back, gain, shift = norm_back(
                pair_sum(chip_rows(partials[turn])), entering[l][turn].astype(F32), w["gain_one"], mask, width
            )
            smalls[turn].update({"gain_one": gain, "shift_one": shift})
            returned.append((grad_middles[turn] + back).astype(BF16))
        sent_back[l] = returned
        if l == 1:
            grads = [r.astype(F32) for r in returned]
        sums = {name: total([small[name] for small in smalls]) for name in smalls[0]}

        def feature_sum(name):
            return sums[name].reshape(chips, part_pad)[:, :part] * once

        own_head = (jnp.arange(HL * HD) >= HD) | (quarter == 0)
        q_sum = sums["packed"][: HL * HD]
        v_sum = sums["packed"][2 * V_LANES : 2 * V_LANES + HL * HD]
        qv_sum = jnp.stack(
            [
                lax.dynamic_update_slice_in_dim(
                    jnp.zeros((H * HD,), F32), jnp.where(own_head, s, 0.0), quarter * HSTEP * HD, axis=0
                )
                for s in (q_sum, v_sum)
            ]
        ).reshape(chips, -1)
        up_sum = sums["up_bias"].reshape(all_groups, 1, 1, hid_pad)[..., :hid]
        at_x = jnp.arange(2)[None, :, None, None] == x_index
        at_c = jnp.arange(2)[None, None, :, None] == core
        up_sum = jnp.where(at_x & at_c, up_sum, 0.0).reshape(chips, -1)
        small_cols = jnp.concatenate(
            [qv_sum, feature_sum("out_bias"), up_sum]
            + [feature_sum(name) for name in ("down_bias", "gain_one", "shift_one", "gain_two", "shift_two")],
            axis=1,
        ).astype(BF16)
        small_cols = jnp.pad(small_cols, ((0, 0), (0, P_LANES - small_total)))[:, None, :]
        d_qkv = d_qkv.reshape(chips, part_pad, P_LANES)
        at_row = lax.broadcasted_iota(jnp.int32, (1, part_pad, 1), 1) == part
        d_qkv = jnp.where(at_row, small_cols, d_qkv)
        qkv_done = scattered(d_qkv, 2 * part_pad)
        finished[l] = {"up": up_done, "down": down_done, "qkv": qkv_done, "out": out_done}

    def back_across_pair(value):
        value = value.reshape(2, part_pad, value.shape[-1])
        return in_turn(pick(value, x_index), flip(pick(value, 1 - x_index), PAIR), x_index, 0)

    def own_layer(first, second):
        mine = jnp.where(core == 0, first, second)
        other = flip(jnp.where(core == 0, second, first), "section")
        return [jnp.where(core == 0, mine, other), jnp.where(core == 0, other, mine)]

    up_c = own_layer(*[back_across_pair(finished[l]["up"]) for l in range(2)])
    down_c = own_layer(*[finished[l]["down"].reshape(hid_pad, width_pad) for l in range(2)])
    qkv_c = own_layer(*[back_across_pair(finished[l]["qkv"]) for l in range(2)])
    out_c = own_layer(
        *[jnp.sum(back_across_pair(finished[l]["out"]).astype(F32), axis=0).astype(BF16) for l in range(2)]
    )

    def heads_sum(lanes_of):
        parts = []
        for x in range(2):
            for c in range(2):
                q = 2 * x + c
                piece = lanes_of(qkv_c[c][x, :part].astype(F32))
                own = jnp.arange(HL * HD) >= (0 if q == 0 else HD)
                piece = jnp.where(own[None], piece, 0.0)
                parts.append(jnp.pad(piece, ((0, 0), (HSTEP * q * HD, (H - HL - HSTEP * q) * HD))))
        return total(parts)

    def third(which):
        return lambda piece: piece[:, which * V_LANES : which * V_LANES + HL * HD]

    grad_w_qkv = jnp.concatenate([heads_sum(third(which)) for which in range(3)], axis=1)
    grad_w_out = narrow(jnp.concatenate([out_c[0], out_c[1][:, side - far :]], axis=1), F32)[:part]
    up_parts = jnp.stack(
        [
            jnp.stack(
                [
                    up_c[c][x, :part].reshape(part, all_groups, hid_pad)[..., :hid] for c in range(2)
                ],
                axis=2,
            )
            for x in range(2)
        ],
        axis=2,
    )
    grad_w_up = up_parts.astype(F32).reshape(part, -1)
    grad_w_down = narrow(jnp.concatenate([down_c[0][:hid], down_c[1][:hid]], axis=0), F32)
    small_sum = total([qkv_c[c][x, part, :small_total].astype(F32) for x in range(2) for c in range(2)])
    small_out, at = {}, 0
    for name in SMALL:
        small_out[name] = small_sum[at : at + small_sizes[name]]
        at += small_sizes[name]

    grads_local = [to_blocks(sent_back[l], l) for l in range(2)]
    input_grad = jnp.where(core == 0, grads_local[0], grads_local[1])
    return (
        acts[None],
        input_grad[None],
        grad_w_qkv[None],
        small_out["b_qv"][None],
        grad_w_out[None],
        small_out["out_bias"][None],
        grad_w_up[None],
        small_out["up_bias"][None],
        grad_w_down[None],
        small_out["down_bias"][None],
        small_out["gain_one"][None],
        small_out["shift_one"][None],
        small_out["gain_two"][None],
        small_out["shift_two"][None],
    )


def solution(mesh):
    sections, groups, positions = (mesh.shape[name] for name in ("section", "dp", "seq"))
    devices = mesh.devices.reshape(sections, groups, positions // 2, 2)
    split = jax.sharding.Mesh(devices, ("section", "dp", "y", "x"))
    seq = ("y", "x")
    wide = P("section", ("dp",) + seq, None)
    thin = P("section", ("dp",) + seq)
    rows = P("dp", seq, None)
    in_specs = (rows, rows, P(), P()) + (wide, thin) * 4 + (thin,) * 4
    out_specs = (P("section", "dp", seq, None),) * 2 + (wide, thin) * 4 + (thin,) * 4
    return jax.shard_map(per_device, mesh=split, in_specs=in_specs, out_specs=out_specs, check_vma=False)
```

```python
import functools

import jax
import jax.numpy as jnp
from jax import lax
from jax.experimental import pallas as pl
from jax.experimental.pallas import tpu as pltpu
from jax.sharding import PartitionSpec as P

H = 25
HD = 64
QUARTERS = 4
HL = -(-H // QUARTERS)
HSTEP = (H - HL) // (QUARTERS - 1)
PAIRS = -(-HL // 2)
V_LANES = PAIRS * 2 * HD
P_LANES = 3 * V_LANES
ROW_BLOCK = 256
F32 = jnp.float32
BF16 = jnp.bfloat16


def round_up(value, by):
    return -(-value // by) * by


def lane_map_kernel(places, x_ref, o_ref):
    width, wide = x_ref.shape[1], o_ref.shape[1]
    for at in range(0, wide, 128):
        end = min(at + 128, wide)
        column = at + lax.broadcasted_iota(jnp.int32, (128, end - at), 1)
        source = places.of(column)
        total = None
        for low in sorted({p // 128 * 128 for p in (places(j) for j in range(at, end)) if p >= 0}):
            high = min(low + 128, width)
            row = low + lax.broadcasted_iota(jnp.int32, (high - low, end - at), 0)
            chosen = (row == source[: high - low]).astype(BF16)
            term = jnp.dot(x_ref[:, low:high], chosen, preferred_element_type=F32)
            total = term if total is None else total + term
        o_ref[:, at:end] = total.astype(o_ref.dtype)


class Spread:
    def __init__(self, part, part_pad):
        self.part, self.part_pad = part, part_pad

    def __call__(self, j):
        return j // self.part_pad * self.part + j % self.part_pad if j % self.part_pad < self.part else -1

    def of(self, j):
        inside = lax.rem(j, self.part_pad)
        return jnp.where(inside < self.part, lax.div(j, self.part_pad) * self.part + inside, -1)


class Gather:
    def __init__(self, part, part_pad):
        self.part, self.part_pad = part, part_pad

    def __call__(self, j):
        return j // self.part * self.part_pad + j % self.part

    def of(self, j):
        return lax.div(j, self.part) * self.part_pad + lax.rem(j, self.part)


def lane_map(value, places, wide, dtype=BF16):
    shape = value.shape[:-1] + (wide,)
    flat = value.reshape(-1, value.shape[-1])
    rows = flat.shape[0]
    block = rows if rows % 256 else 256
    result = pl.pallas_call(
        functools.partial(lane_map_kernel, places),
        grid=(rows // block,),
        in_specs=[pl.BlockSpec((block, flat.shape[1]), lambda i: (i, 0))],
        out_specs=pl.BlockSpec((block, wide), lambda i: (i, 0)),
        out_shape=jax.ShapeDtypeStruct((rows, wide), dtype),
        compiler_params=pltpu.CompilerParams(vmem_limit_bytes=32 * 2**20),
        cost_estimate=FREE,
        name="lane_map",
    )(flat)
    return result.reshape(shape)


NT = (((1,), (1,)), ((), ()))
TN = (((0,), (0,)), ((), ()))
FREE = pl.CostEstimate(flops=0, bytes_accessed=0, transcendentals=0)


def on_each_part(info_ref, parts, body):
    if parts == 1:
        body(0)
        return
    for part in range(parts):
        pl.when(info_ref[info_ref.shape[0] - 1] == part)(functools.partial(body, part))


def heads_of_pair(body):
    if HL % 2 == 0:
        body((0, 1))
        return
    last = pl.program_id(1) == PAIRS - 1
    pl.when(jnp.logical_not(last))(functools.partial(body, (0, 1)))
    pl.when(last)(functools.partial(body, (0,)))


def attn_fwd_kernel(info_ref, q_ref, k_ref, v_ref, o_ref, lse_ref):
    total, rows = k_ref.shape[0], o_ref.shape[0]
    length = info_ref[pl.program_id(0)]
    block = min(ROW_BLOCK, rows)
    lower = lax.broadcasted_iota(jnp.int32, (block, 2 * HD), 1) < HD
    keep = jnp.where(lax.broadcasted_iota(jnp.int32, (total, 1), 0) < length, 0.0, -1e30)

    def body(heads, half):
        for i in range(rows // block):
            first = half * rows + i * block
            end = first + block
            key = lax.broadcasted_iota(jnp.int32, (end, block), 0)
            query = lax.broadcasted_iota(jnp.int32, (end, block), 1) + first
            probs = []
            for a in heads:
                mine = lower if a == 0 else jnp.logical_not(lower)
                q = jnp.where(mine, q_ref[first:end, :] * jnp.asarray(HD**-0.5, BF16), jnp.zeros((), BF16))
                scores = lax.dot_general(k_ref[:end, :], q, NT, preferred_element_type=F32) + keep[:end]
                scores = jnp.where(key <= query, scores, -1e30)
                top = jnp.max(scores, axis=0, keepdims=True)
                weights = jnp.exp(scores - top)
                below = jnp.sum(weights, axis=0, keepdims=True)
                lse_ref[a : a + 1, i * block : (i + 1) * block] = top + jnp.log(below)
                probs.append((weights * (1.0 / below)).astype(BF16))
            parts = [lax.dot_general(p, v_ref[:end, :], TN, preferred_element_type=F32) for p in probs]
            upper = parts[1] if len(heads) == 2 else jnp.zeros_like(parts[0])
            o_ref[i * block : (i + 1) * block, :] = jnp.where(lower, parts[0], upper).astype(BF16)

    lse_ref[...] = jnp.zeros_like(lse_ref)
    heads_of_pair(lambda heads: on_each_part(info_ref, total // rows, functools.partial(body, heads)))


def pair_spec(rows, lanes, offset=0):
    return pl.BlockSpec((None, rows, lanes), lambda i, j: (i, 0, j + offset))


def stats_spec(rows):
    return pl.BlockSpec((None, None, 2, rows), lambda i, j: (i, j, 0, 0))


def attn_forward(packed, info, rows):
    count, total, _ = packed.shape
    return pl.pallas_call(
        attn_fwd_kernel,
        grid=(count, PAIRS),
        in_specs=[
            pl.BlockSpec(memory_space=pltpu.SMEM),
            pair_spec(total, 2 * HD),
            pair_spec(total, 2 * HD, PAIRS),
            pair_spec(total, 2 * HD, 2 * PAIRS),
        ],
        out_specs=[pair_spec(rows, 2 * HD), stats_spec(rows)],
        out_shape=[
            jax.ShapeDtypeStruct((count, rows, V_LANES), BF16),
            jax.ShapeDtypeStruct((count, PAIRS, 2, rows), F32),
        ],
        compiler_params=pltpu.CompilerParams(vmem_limit_bytes=48 * 2**20),
        cost_estimate=FREE,
        name="attn_fwd",
    )(info, packed, packed, packed)


def attn_bwd_kernel(info_ref, q_ref, k_ref, v_ref, g_ref, o_ref, lse_ref, out_ref):
    total, rows = k_ref.shape[0], g_ref.shape[0]
    block = min(2 * ROW_BLOCK, rows)
    count = total // block
    pair = pl.program_id(1)
    length = info_ref[pl.program_id(0)]
    lane = lax.broadcasted_iota(jnp.int32, (block, 2 * HD), 1)
    key = lax.broadcasted_iota(jnp.int32, (block, block), 0)
    query = lax.broadcasted_iota(jnp.int32, (block, block), 1)
    key_row = lax.broadcasted_iota(jnp.int32, (block, 1), 0)

    def body(heads, half):
        nothing = jnp.zeros((block, 2 * HD), F32)
        dq, dk, dv = {}, {}, {}
        for i in range(rows // block):
            at = slice(i * block, (i + 1) * block)
            place = half * rows // block + i
            g = g_ref[at, :]
            product = g.astype(F32) * o_ref[at, :].astype(F32)
            mine = {}
            for a in heads:
                lanes = (lane < HD) if a == 0 else (lane >= HD)
                inner = lax.dot_general(
                    jnp.ones((8, 2 * HD), F32),
                    jnp.where(lanes, product, 0.0),
                    NT,
                    preferred_element_type=F32,
                    precision=lax.Precision.HIGHEST,
                )[0:1]
                q = q_ref[place * block : (place + 1) * block, :] * jnp.asarray(HD**-0.5, BF16)
                q = jnp.where(lanes, q, jnp.zeros_like(q))
                mine[a] = (q, jnp.where(lanes, g, jnp.zeros_like(g)), inner, lse_ref[a : a + 1, at])
            for j in range(place + 1):
                keys = slice(j * block, (j + 1) * block)
                keep = jnp.where(key_row < length - j * block, 0.0, -1e30)
                for a in heads:
                    q, g_mine, inner, lse = mine[a]
                    k = k_ref[keys, :]
                    scores = lax.dot_general(k, q, NT, preferred_element_type=F32) + keep
                    if j == place:
                        scores = jnp.where(key <= query, scores, -1e30)
                    probs = jnp.exp(scores - lse)
                    gprobs = lax.dot_general(v_ref[keys, :], g_mine, NT, preferred_element_type=F32)
                    gscores = (probs * (gprobs - inner)).astype(BF16)
                    dq[a, place] = dq.get((a, place), 0.0) + lax.dot_general(
                        gscores, k, TN, preferred_element_type=F32
                    )
                    dk[a, j] = dk.get((a, j), 0.0) + jnp.dot(gscores, q, preferred_element_type=F32)
                    dv[j] = dv.get(j, 0.0) + jnp.dot(probs.astype(BF16), g_mine, preferred_element_type=F32)
        for j in range(count):
            at = slice(j * block, (j + 1) * block)
            low, high = heads[0], heads[-1]
            dq_both = jnp.where(lane < HD, dq.get((low, j), nothing), dq.get((high, j), nothing)) * HD**-0.5
            dk_both = jnp.where(lane < HD, dk.get((low, j), nothing), dk.get((high, j), nothing))
            for which, value in enumerate((dq_both, dk_both, dv.get(j, nothing))):
                start = pl.multiple_of(which * V_LANES + pair * 2 * HD, 2 * HD)
                out_ref[at, pl.ds(start, 2 * HD)] = value.astype(BF16)

    heads_of_pair(lambda heads: on_each_part(info_ref, total // rows, functools.partial(body, heads)))


def attn_backward(packed, grad, attended, lse, info):
    (count, total, _), rows = packed.shape, grad.shape[1]
    return pl.pallas_call(
        attn_bwd_kernel,
        grid=(count, PAIRS),
        in_specs=[
            pl.BlockSpec(memory_space=pltpu.SMEM),
            pair_spec(total, 2 * HD),
            pair_spec(total, 2 * HD, PAIRS),
            pair_spec(total, 2 * HD, 2 * PAIRS),
            pair_spec(rows, 2 * HD),
            pair_spec(rows, 2 * HD),
            stats_spec(rows),
        ],
        out_specs=pl.BlockSpec((None, total, P_LANES), lambda i, j: (i, 0, 0)),
        out_shape=jax.ShapeDtypeStruct((count, total, P_LANES), BF16),
        compiler_params=pltpu.CompilerParams(vmem_limit_bytes=56 * 2**20),
        cost_estimate=FREE,
        name="attn_bwd",
    )(info, packed, packed, packed, grad, attended, lse)


PAIR = "x"


def flip(value, axis):
    return lax.ppermute(value, axis, [(0, 1), (1, 0)])


def in_turn(mine, other, mine_at, axis):
    shape = [1] * mine.ndim
    shape[axis] = 2
    place = lax.broadcasted_iota(jnp.int32, tuple(shape), axis)
    return jnp.where(place == mine_at, mine, other)


def pick(value, at, axis=0):
    return lax.dynamic_slice_in_dim(value, at, 1, axis=axis)


def there(*tokens):
    result = None
    for leaf in jax.tree.leaves(tokens):
        first = lax.slice(leaf, (0,) * leaf.ndim, (1,) * leaf.ndim).reshape(())
        result = (first == first) if result is None else result & (first == first)
    return result


def tied(value, *tokens):
    if not jax.tree.leaves(tokens):
        return value
    return value + jnp.where(there(tokens), 0, 1).astype(value.dtype)


def rows_of_both(own):
    count, rows, width = own.shape
    both = in_turn(own[:, None], flip(own, "section")[:, None], lax.axis_index("section"), 1)
    return both.reshape(count, 2 * rows, width)


def chip_rows(partial):
    count, rows, width = partial.shape
    core = lax.axis_index("section")
    split = partial.reshape(count, 2, rows // 2, width)
    other = flip(pick(split, 1 - core, 1)[:, 0], "section")
    return (pick(split, core, 1)[:, 0].astype(F32) + other.astype(F32)).astype(BF16)


class PairSum:
    def __init__(self):
        self.before = ()

    def hold(self, value):
        self.before += (value,)

    def __call__(self, chip):
        arrived = flip(tied(chip, self.before), PAIR)
        self.before = (arrived,)
        return chip.astype(F32) + arrived.astype(F32)


def dot(a, b):
    flat = jnp.dot(a.reshape(-1, a.shape[-1]), b, preferred_element_type=F32)
    return flat.reshape(a.shape[:-1] + (b.shape[1],))


def dot_t(a, b):
    flat = lax.dot_general(a.reshape(-1, a.shape[-1]), b, NT, preferred_element_type=F32)
    return flat.reshape(a.shape[:-1] + (b.shape[0],))


def dot_0(a, b):
    return lax.dot_general(a.reshape(-1, a.shape[-1]), b.reshape(-1, b.shape[-1]), TN, preferred_element_type=F32)


def row_sum(value):
    return jnp.sum(value.astype(F32), axis=(0, 1))


def gelu_parts(u):
    t = jnp.tanh(0.7978845608 * (u + 0.044715 * u * u * u))
    return t


def gelu(u):
    return 0.5 * u * (1.0 + gelu_parts(u))


def gelu_slope(u):
    t = gelu_parts(u)
    return 0.5 * (1.0 + t) + 0.5 * u * (1.0 - t * t) * 0.7978845608 * (1.0 + 3 * 0.044715 * u * u)


def norm_stats(rows, mask, width):
    average = jnp.sum(rows, axis=-1, keepdims=True) / width
    centered = (rows - average) * mask
    variance = jnp.sum(centered * centered, axis=-1, keepdims=True) / width
    scale = lax.rsqrt(variance + 1e-05)
    return centered * scale, scale


def norm_back(grad, rows, gain, mask, width):
    hat, scale = norm_stats(rows, mask, width)
    inner = grad * gain
    mean_one = jnp.sum(inner, axis=-1, keepdims=True) / width
    mean_two = jnp.sum(inner * hat, axis=-1, keepdims=True) / width
    back = scale * (inner - mean_one - hat * mean_two) * mask
    return back, row_sum(grad * hat), row_sum(grad * mask)


def whole_sequence(packed):
    parts = lax.axis_size("y")
    if parts == 2:
        other = lax.ppermute(packed[..., V_LANES:], "y", [(0, 1)])
        other = jnp.pad(other, ((0, 0), (0, 0), (V_LANES, 0)))
        both = in_turn(packed[:, None], other[:, None], lax.axis_index("y"), 1)
    else:
        both = lax.all_gather(packed, "y", axis=1)
    return both.reshape(packed.shape[0], parts * packed.shape[1], packed.shape[2])


def own_rows(grad):
    parts = lax.axis_size("y")
    rows = grad.shape[1] // parts
    if parts != 2:
        return lax.psum_scatter(grad, "y", scatter_dimension=1, tiled=True)
    other = lax.ppermute(grad[:, :rows, V_LANES:], "y", [(1, 0)])
    other = jnp.pad(other, ((0, 0), (0, 0), (V_LANES, 0)))
    own = lax.dynamic_slice_in_dim(grad, lax.axis_index("y") * rows, rows, axis=1)
    return (own.astype(F32) + other.astype(F32)).astype(BF16)


def project_stage(rows, w, mask, width):
    hat, _ = norm_stats(rows.astype(F32), mask, width)
    normed = rows_of_both((hat * w["gain_one"] + w["shift_one"]).astype(BF16))
    packed = (dot(normed, w["qkv"]) + w["qkv_bias"]).astype(BF16)
    return normed, whole_sequence(packed)


def attend_stage(normed, packed, w, info):
    attended, lse = attn_forward(packed, info, normed.shape[1])
    return dot(attended, w["out"]).astype(BF16), (normed, packed, attended, lse)


def ffn_stage(middle, w, mask, width):
    hat, _ = norm_stats(middle, mask, width)
    normed = rows_of_both((hat * w["gain_two"] + w["shift_two"]).astype(BF16))
    upward = dot(normed, w["up"]) + w["up_bias"]
    hidden = gelu(upward).astype(BF16)
    partial = dot(hidden, w["down"]).astype(BF16)
    return partial, (normed, upward.astype(BF16), hidden)


def ffn_back_stage(grad_out, kept, w, token=()):
    normed, upward, hidden = kept
    grad_down = tied(grad_out.astype(BF16), token)
    b_down = row_sum(grad_down)
    grad_down = rows_of_both(grad_down)
    grad_up = (dot_t(grad_down, w["down"]) * gelu_slope(upward.astype(F32))).astype(BF16)
    b_up = row_sum(grad_up)
    partial = dot_t(grad_up, w["up"]).astype(BF16)
    return partial, {"down_bias": b_down, "up_bias": b_up}, {"down": (hidden, grad_down), "up": (normed, grad_up)}


def branch_stage(grad_middle, kept, token=()):
    grad_branch = tied(grad_middle.astype(BF16), token)
    return rows_of_both(grad_branch), {"out_bias": row_sum(grad_branch)}


def attend_back_stage(grad_branch, kept, w, info):
    normed, packed, attended, lse = kept
    grad_attended = dot_t(grad_branch, w["out"]).astype(BF16)
    return attn_backward(packed, grad_attended, attended, lse, info)


def project_back_stage(grad_packed, kept, w):
    grad_packed = own_rows(grad_packed)
    b_packed = row_sum(grad_packed)
    partial = dot_t(grad_packed, w["qkv"]).astype(BF16)
    return partial, {"packed": b_packed}, {"qkv": (kept[0], grad_packed)}


SMALL = ("b_qv", "out_bias", "up_bias", "down_bias", "gain_one", "shift_one", "gain_two", "shift_two")


def per_device(
    inputs,
    cotangent,
    lengths,
    dealing,
    query_key_value_weight,
    b_qv,
    attention_out_weight,
    attention_out_bias,
    up_weight,
    up_bias,
    down_weight,
    down_bias,
    gain_one,
    shift_one,
    gain_two,
    shift_two,
):
    micro, block_rows, width = inputs.shape
    dp_count, y_count = lax.axis_size("dp"), lax.axis_size("y")
    chips = 2 * dp_count * y_count
    all_groups = dp_count * y_count
    core, dp_index = lax.axis_index("section"), lax.axis_index("dp")
    x_index, y_index = lax.axis_index("x"), lax.axis_index("y")
    quarter = 2 * x_index + core
    part = query_key_value_weight.shape[1]
    part_pad = round_up(part + 1, 8)
    width_pad = chips * part_pad
    hid = down_weight.shape[1] // 2
    hid_pad = round_up(hid, 8)
    while all_groups * hid_pad % 128:
        hid_pad += 8

    lane = lax.broadcasted_iota(jnp.int32, (1, width_pad), 1)
    mask = (lane % part_pad < part).astype(F32)
    local = lax.broadcasted_iota(jnp.int32, (V_LANES, width_pad), 0)
    column = lax.broadcasted_iota(jnp.int32, (V_LANES, width_pad), 1)
    whole_row = local + quarter * HSTEP * HD
    own_local = (local < HL * HD) & ((local >= HD) | (quarter == 0))
    placed = ((column == whole_row // part * part_pad + whole_row % part) & own_local).astype(BF16)
    side = round_up(width_pad // 2, 128)
    far = width_pad - side

    def widen(value):
        return lane_map(value, Spread(part, part_pad), width_pad)

    def narrow(value, dtype=BF16):
        return lane_map(value.astype(BF16), Gather(part, part_pad), width, dtype)

    def pad_rows(value, rows):
        return jnp.pad(value, ((0, rows - value.shape[0]), (0, 0)))

    small_in = dict(
        zip(SMALL, (b_qv, attention_out_bias, up_bias, down_bias, gain_one, shift_one, gain_two, shift_two))
    )
    small_sizes = {name: value.shape[1] for name, value in small_in.items()}
    small_row = jnp.concatenate([small_in[name][0] for name in SMALL])
    small_total = small_row.shape[0]

    shard = query_key_value_weight[0].reshape(part, 3, H, HD)

    out_wide = pad_rows(widen(attention_out_weight[0]), part_pad)
    out_pieces = jnp.stack([jnp.stack([out_wide[:, at : at + side]] * 2) for at in (0, far)])

    def attn_piece(q):
        from_head = HSTEP * q
        heads = shard[:, :, from_head : from_head + HL]
        body = jnp.pad(heads.reshape(part, 3, HL * HD), ((0, 0), (0, 0), (0, V_LANES - HL * HD)))
        body = body.reshape(part, P_LANES)
        row = jnp.pad(small_row, (0, P_LANES - small_total))[None]
        return pad_rows(jnp.concatenate([body, row], axis=0), part_pad)

    up_shard = up_weight[0].reshape(part, all_groups, 2, 2, hid)

    def up_piece(q):
        body = up_shard[:, :, q // 2, q % 2]
        body = jnp.pad(body, ((0, 0), (0, 0), (0, hid_pad - hid))).reshape(part, all_groups * hid_pad)
        return pad_rows(body, part_pad)

    attn_pieces = jnp.stack([jnp.stack([attn_piece(2 * x + c) for x in range(2)]) for c in range(2)])
    up_pieces = jnp.stack([jnp.stack([up_piece(2 * x + c) for x in range(2)]) for c in range(2)])
    down_wide = widen(down_weight[0]).reshape(2, hid, width_pad)
    down_pieces = jnp.pad(down_wide, ((0, 0), (0, hid_pad - hid), (0, 0)))

    def by_layer(pieces):
        mine, other = pick(pieces, core)[0], flip(pick(pieces, 1 - core)[0], "section")
        return [jnp.where(core == 0, mine, other), jnp.where(core == 0, other, mine)]

    def across_pair(pieces):
        both = in_turn(pick(pieces, x_index), flip(pick(pieces, 1 - x_index), PAIR), x_index, 0)
        return both.reshape(2 * part_pad, both.shape[-1])

    groups = ("dp", "y")
    down_l = by_layer(down_pieces)
    attn_l = [across_pair(pieces) for pieces in by_layer(jnp.concatenate([attn_pieces, out_pieces], axis=-1))]
    up_l = [across_pair(pieces) for pieces in by_layer(up_pieces)]
    def gather(piece, *tokens):
        return lax.all_gather(tied(piece, tokens), groups, axis=0)

    down_first, attn_first = gather(down_l[0]), gather(attn_l[0])
    up_first = gather(up_l[0], down_first)
    weights = []

    def layer_of(attn_all, up_all, down_all):
        if attn_all is None:
            return {"down": down_all.reshape(all_groups * hid_pad, width_pad)}
        if isinstance(attn_all, tuple):
            qkv_all, out_all = (piece.reshape(width_pad, -1) for piece in attn_all)
        else:
            attn_all = attn_all.reshape(width_pad, P_LANES + side)
            qkv_all, out_all = attn_all[:, :P_LANES], attn_all[:, P_LANES:]
        small_all = qkv_all.reshape(chips, part_pad, P_LANES)[:, part, :small_total]
        pieces, at = {}, 0
        for name in SMALL:
            pieces[name] = small_all[:, at : at + small_sizes[name]]
            at += small_sizes[name]

        def feature(name):
            return jnp.pad(pieces[name].astype(F32), ((0, 0), (0, part_pad - part))).reshape(1, width_pad)

        qv = pieces["b_qv"].astype(F32).reshape(2, H * HD)
        own_qv = lax.dynamic_slice_in_dim(qv, quarter * HSTEP * HD, HL * HD, axis=1)
        own_qv = jnp.pad(own_qv, ((0, 0), (0, V_LANES - HL * HD)))
        qkv_bias = jnp.concatenate([own_qv[0], jnp.zeros((V_LANES,), F32), own_qv[1]])[None]
        ups = pieces["up_bias"].astype(F32).reshape(all_groups, 2, 2, hid)
        up_mine = lax.dynamic_index_in_dim(
            lax.dynamic_index_in_dim(ups, x_index, 1, keepdims=False), core, 1, keepdims=False
        )
        up_bias_row = jnp.pad(up_mine, ((0, 0), (0, hid_pad - hid))).reshape(1, all_groups * hid_pad)
        sides = in_turn(out_all[None], flip(out_all, "section")[None], core, 0)
        out_both = jnp.concatenate([sides[0], sides[1, :, side - far :]], axis=1)
        out_mine = dot(placed, out_both).astype(BF16)
        return {
                "qkv": qkv_all.reshape(width_pad, P_LANES),
                "qkv_bias": qkv_bias,
                "out": out_mine,
                "out_bias": feature("out_bias"),
                "up": up_all.reshape(width_pad, all_groups * hid_pad),
                "up_bias": up_bias_row,
                "down": None if down_all is None else down_all.reshape(all_groups * hid_pad, width_pad),
                "down_bias": feature("down_bias"),
                "gain_one": feature("gain_one"),
                "shift_one": feature("shift_one"),
                "gain_two": feature("gain_two"),
                "shift_two": feature("shift_two"),
        }

    rounds = [range(0, micro - micro // 2), range(micro - micro // 2, micro)]
    turns = range(len(rounds))
    CORE_X = ("section", "x")

    def to_rounds(value):
        rows = jnp.where(core == x_index, value, lax.ppermute(value, CORE_X, [(0, 1), (3, 2)]))
        rows = widen(rows)
        return [rows[r.start : r.stop] for r in rounds]

    def to_blocks(value, layer):
        rows = narrow(jnp.concatenate(value, axis=0))
        pairs = [(0, 2 * layer), (3, 2 * layer + 1), (1, 2 - 2 * layer), (2, 3 - 2 * layer)]
        return lax.ppermute(rows, CORE_X, pairs)

    own_lengths = lax.dynamic_slice_in_dim(lengths, dp_index * micro, micro)
    positions = (2 * y_index + core) * block_rows + jnp.arange(block_rows, dtype=jnp.int32)
    turn_info = [jnp.concatenate([own_lengths[r.start : r.stop], y_index[None].astype(jnp.int32)]) for r in rounds]

    start_rows = to_rounds(inputs)
    grad_rows = to_rounds(tied(cotangent, up_first))

    kept_attn = [[None] * len(rounds) for _ in range(2)]
    kept_ffn = [[None] * len(rounds) for _ in range(2)]
    middles = [[None] * len(rounds) for _ in range(2)]
    entering = [start_rows, None]
    pair_sum = PairSum()
    outputs = [None, None]
    layers = [layer_of(attn_first, up_first, down_first), None]
    for l in range(2):
        w = layers[l]
        partials, chip = [None] * len(rounds), [None] * len(rounds)
        projected = [None] * len(rounds)
        for turn in reversed(turns):
            projected[turn] = project_stage(entering[l][turn], w, mask, width)
        if l == 0:
            out_second = gather(attn_l[1][:, P_LANES:], projected[0][1], up_first)
            qkv_second = gather(attn_l[1][:, :P_LANES], projected[0][1], up_first)
        else:
            weights.append(gather(down_l[1], projected[0][1]))
            layers[1].update(layer_of(None, None, weights[-1]))
        for turn in turns:
            partials[turn], kept_attn[l][turn] = attend_stage(*projected[turn], w, turn_info[turn])
        for turn in turns:
            middles[l][turn] = entering[l][turn].astype(F32) + pair_sum(chip_rows(partials[turn])) + w["out_bias"]
            partials[turn], kept_ffn[l][turn] = ffn_stage(middles[l][turn], w, mask, width)
            if l == 0 and turn == 0:
                up_second = gather(up_l[1], partials[turn])
                layers[1] = layer_of((qkv_second, out_second), up_second, None)
        outputs[l] = [
            (middles[l][turn] + pair_sum(chip_rows(partials[turn])) + w["down_bias"]).astype(BF16) for turn in turns
        ]
        if l == 0:
            entering[1] = outputs[0]

    def deal(token):
        acts_local = [to_blocks(outputs[l], l) for l in range(2)]
        acts_local = jnp.where(core == 0, acts_local[0], acts_local[1])
        total_seqs = dealing.shape[0]
        numbers = jnp.arange(total_seqs, dtype=jnp.int32)
        position = jnp.sum(jnp.where(dealing[:, None] == numbers[None, :], numbers[:, None], 0), axis=0)
        target = lax.dynamic_slice_in_dim(position, dp_index * micro, micro) // micro
        anchor = lax.dynamic_slice_in_dim(dealing, dp_index * micro, micro) // micro
        dealt = []
        for d in range(dp_count):
            dest = dp_index ^ d
            send = acts_local[0]
            for i in range(1, micro):
                send = jnp.where(target[i] == dest, acts_local[i], send)
            send = tied(send, token)
            if d:
                send = lax.ppermute(send, "dp", [(i, i ^ d) for i in range(dp_count)])
            dealt.append(send)
        result = []
        for j in range(micro):
            offset = anchor[j] ^ dp_index
            chosen = dealt[0]
            for d in range(1, dp_count):
                chosen = jnp.where(offset == d, dealt[d], chosen)
            result.append(chosen)
        return jnp.stack(result)

    def total(values):
        return functools.reduce(jnp.add, values)

    def product(operands):
        return total([dot_0(a, b) for a, b in operands]).astype(BF16)

    once = (x_index == 0).astype(F32)
    valid = [positions[None] < own_lengths[r.start : r.stop, None] for r in rounds]
    grads = [jnp.where(valid[turn][..., None], grad_rows[turn].astype(F32), 0.0) for turn in turns]

    def scattered(value, rows):
        value = value.reshape(all_groups, rows, value.shape[-1])
        return lax.psum_scatter(value, groups, scatter_dimension=0, tiled=False)

    finished = [None, None]
    token = ()
    sent_back = [None, None]
    for l in (1, 0):
        w = layers[l]
        smalls, operands, partials = [{} for _ in turns], [{} for _ in turns], [None] * len(rounds)
        for turn in turns:
            partials[turn], small, ops = ffn_back_stage(grads[turn], kept_ffn[l][turn], w, token)
            smalls[turn].update(small)
            operands[turn].update(ops)
        d_down = product([ops["down"] for ops in operands])
        d_up = product([ops["up"] for ops in operands])
        token = (d_down, d_up)
        down_done = scattered(d_down, hid_pad)
        up_done = scattered(d_up, 2 * part_pad)
        grad_middles = [None] * len(rounds)
        for turn in turns:
            if l == 0 and turn == 1:
                pair_sum.hold(finished[1]["up"])
            back, gain, shift = norm_back(
                pair_sum(chip_rows(partials[turn])), middles[l][turn], w["gain_two"], mask, width
            )
            smalls[turn].update({"gain_two": gain, "shift_two": shift})
            grad_middles[turn] = grads[turn] + back
        branches = [None] * len(rounds)
        for turn in turns:
            branches[turn], small = branch_stage(grad_middles[turn], kept_attn[l][turn], token)
            smalls[turn].update(small)
            operands[turn]["out"] = (kept_attn[l][turn][2], branches[turn])
        if l == 0:
            acts = deal(tuple(branches))
        d_out = dot_0(placed, product([ops["out"] for ops in operands])).astype(BF16)
        out_own = lax.dynamic_slice_in_dim(d_out, core * far, side, axis=1)
        out_other = flip(lax.dynamic_slice_in_dim(d_out, (1 - core) * far, side, axis=1), "section")
        d_out = (out_own.astype(F32) + out_other.astype(F32)).astype(BF16)
        out_done = scattered(d_out, 2 * part_pad)
        grad_packed, before = [None] * len(rounds), ()
        for turn in reversed(turns):
            grad_packed[turn] = attend_back_stage(
                branches[turn], kept_attn[l][turn], w, turn_info[turn] + jnp.where(there(before), 0, 1)
                if before
                else turn_info[turn]
            )
            before = (grad_packed[turn],)
        for turn in turns:
            partials[turn], small, ops = project_back_stage(grad_packed[turn], kept_attn[l][turn], w)
            smalls[turn].update(small)
            operands[turn].update(ops)
        d_qkv = product([ops["qkv"] for ops in operands])
        token = (d_qkv, out_done)
        returned = []
        for turn in turns:
            if l == 1 and turn == 1:
                pair_sum.hold(down_done)
            if l == 0 and turn == 1:
                pair_sum.hold((acts, finished[1]["qkv"]))
            back, gain, shift = norm_back(
                pair_sum(chip_rows(partials[turn])), entering[l][turn].astype(F32), w["gain_one"], mask, width
            )
            smalls[turn].update({"gain_one": gain, "shift_one": shift})
            returned.append((grad_middles[turn] + back).astype(BF16))
        sent_back[l] = returned
        if l == 1:
            grads = [r.astype(F32) for r in returned]
        sums = {name: total([small[name] for small in smalls]) for name in smalls[0]}

        def feature_sum(name):
            return sums[name].reshape(chips, part_pad)[:, :part] * once

        own_head = (jnp.arange(HL * HD) >= HD) | (quarter == 0)
        q_sum = sums["packed"][: HL * HD]
        v_sum = sums["packed"][2 * V_LANES : 2 * V_LANES + HL * HD]
        qv_sum = jnp.stack(
            [
                lax.dynamic_update_slice_in_dim(
                    jnp.zeros((H * HD,), F32), jnp.where(own_head, s, 0.0), quarter * HSTEP * HD, axis=0
                )
                for s in (q_sum, v_sum)
            ]
        ).reshape(chips, -1)
        up_sum = sums["up_bias"].reshape(all_groups, 1, 1, hid_pad)[..., :hid]
        at_x = jnp.arange(2)[None, :, None, None] == x_index
        at_c = jnp.arange(2)[None, None, :, None] == core
        up_sum = jnp.where(at_x & at_c, up_sum, 0.0).reshape(chips, -1)
        small_cols = jnp.concatenate(
            [qv_sum, feature_sum("out_bias"), up_sum]
            + [feature_sum(name) for name in ("down_bias", "gain_one", "shift_one", "gain_two", "shift_two")],
            axis=1,
        ).astype(BF16)
        small_cols = jnp.pad(small_cols, ((0, 0), (0, P_LANES - small_total)))[:, None, :]
        d_qkv = d_qkv.reshape(chips, part_pad, P_LANES)
        at_row = lax.broadcasted_iota(jnp.int32, (1, part_pad, 1), 1) == part
        d_qkv = jnp.where(at_row, small_cols, d_qkv)
        qkv_done = scattered(d_qkv, 2 * part_pad)
        finished[l] = {"up": up_done, "down": down_done, "qkv": qkv_done, "out": out_done}

    def back_across_pair(value):
        value = value.reshape(2, part_pad, value.shape[-1])
        return in_turn(pick(value, x_index), flip(pick(value, 1 - x_index), PAIR), x_index, 0)

    def own_layer(first, second):
        mine = jnp.where(core == 0, first, second)
        other = flip(jnp.where(core == 0, second, first), "section")
        return [jnp.where(core == 0, mine, other), jnp.where(core == 0, other, mine)]

    up_c = own_layer(*[back_across_pair(finished[l]["up"]) for l in range(2)])
    down_c = own_layer(*[finished[l]["down"].reshape(hid_pad, width_pad) for l in range(2)])
    qkv_c = own_layer(*[back_across_pair(finished[l]["qkv"]) for l in range(2)])
    out_c = own_layer(
        *[jnp.sum(back_across_pair(finished[l]["out"]).astype(F32), axis=0).astype(BF16) for l in range(2)]
    )

    def heads_sum(lanes_of):
        parts = []
        for x in range(2):
            for c in range(2):
                q = 2 * x + c
                piece = lanes_of(qkv_c[c][x, :part].astype(F32))
                own = jnp.arange(HL * HD) >= (0 if q == 0 else HD)
                piece = jnp.where(own[None], piece, 0.0)
                parts.append(jnp.pad(piece, ((0, 0), (HSTEP * q * HD, (H - HL - HSTEP * q) * HD))))
        return total(parts)

    def third(which):
        return lambda piece: piece[:, which * V_LANES : which * V_LANES + HL * HD]

    grad_w_qkv = jnp.concatenate([heads_sum(third(which)) for which in range(3)], axis=1)
    grad_w_out = narrow(jnp.concatenate([out_c[0], out_c[1][:, side - far :]], axis=1), F32)[:part]
    up_parts = jnp.stack(
        [
            jnp.stack(
                [
                    up_c[c][x, :part].reshape(part, all_groups, hid_pad)[..., :hid] for c in range(2)
                ],
                axis=2,
            )
            for x in range(2)
        ],
        axis=2,
    )
    grad_w_up = up_parts.astype(F32).reshape(part, -1)
    grad_w_down = narrow(jnp.concatenate([down_c[0][:hid], down_c[1][:hid]], axis=0), F32)
    small_sum = total([qkv_c[c][x, part, :small_total].astype(F32) for x in range(2) for c in range(2)])
    small_out, at = {}, 0
    for name in SMALL:
        small_out[name] = small_sum[at : at + small_sizes[name]]
        at += small_sizes[name]

    grads_local = [to_blocks(sent_back[l], l) for l in range(2)]
    input_grad = jnp.where(core == 0, grads_local[0], grads_local[1])
    return (
        acts[None],
        input_grad[None],
        grad_w_qkv[None],
        small_out["b_qv"][None],
        grad_w_out[None],
        small_out["out_bias"][None],
        grad_w_up[None],
        small_out["up_bias"][None],
        grad_w_down[None],
        small_out["down_bias"][None],
        small_out["gain_one"][None],
        small_out["shift_one"][None],
        small_out["gain_two"][None],
        small_out["shift_two"][None],
    )


def solution(mesh):
    sections, groups, positions = (mesh.shape[name] for name in ("section", "dp", "seq"))
    devices = mesh.devices.reshape(sections, groups, positions // 2, 2)
    split = jax.sharding.Mesh(devices, ("section", "dp", "y", "x"))
    seq = ("y", "x")
    wide = P("section", ("dp",) + seq, None)
    thin = P("section", ("dp",) + seq)
    rows = P("dp", seq, None)
    in_specs = (rows, rows, P(), P()) + (wide, thin) * 4 + (thin,) * 4
    out_specs = (P("section", "dp", seq, None),) * 2 + (wide, thin) * 4 + (thin,) * 4
    return jax.shard_map(per_device, mesh=split, in_specs=in_specs, out_specs=out_specs, check_vma=False)
```

```python
import functools

import jax
import jax.numpy as jnp
from jax import lax
from jax.experimental import pallas as pl
from jax.experimental.pallas import tpu as pltpu
from jax.sharding import PartitionSpec as P

H = 25
HD = 64
QUARTERS = 4
HL = -(-H // QUARTERS)
HSTEP = (H - HL) // (QUARTERS - 1)
PAIRS = -(-HL // 2)
V_LANES = PAIRS * 2 * HD
P_LANES = 3 * V_LANES
ROW_BLOCK = 256
F32 = jnp.float32
BF16 = jnp.bfloat16


def round_up(value, by):
    return -(-value // by) * by


def lane_map_kernel(places, x_ref, o_ref):
    width, wide = x_ref.shape[1], o_ref.shape[1]
    for at in range(0, wide, 128):
        end = min(at + 128, wide)
        column = at + lax.broadcasted_iota(jnp.int32, (128, end - at), 1)
        source = places.of(column)
        total = None
        for low in sorted({p // 128 * 128 for p in (places(j) for j in range(at, end)) if p >= 0}):
            high = min(low + 128, width)
            row = low + lax.broadcasted_iota(jnp.int32, (high - low, end - at), 0)
            chosen = (row == source[: high - low]).astype(BF16)
            term = jnp.dot(x_ref[:, low:high], chosen, preferred_element_type=F32)
            total = term if total is None else total + term
        o_ref[:, at:end] = total.astype(o_ref.dtype)


class Spread:
    def __init__(self, part, part_pad):
        self.part, self.part_pad = part, part_pad

    def __call__(self, j):
        return j // self.part_pad * self.part + j % self.part_pad if j % self.part_pad < self.part else -1

    def of(self, j):
        inside = lax.rem(j, self.part_pad)
        return jnp.where(inside < self.part, lax.div(j, self.part_pad) * self.part + inside, -1)


class Gather:
    def __init__(self, part, part_pad):
        self.part, self.part_pad = part, part_pad

    def __call__(self, j):
        return j // self.part * self.part_pad + j % self.part

    def of(self, j):
        return lax.div(j, self.part) * self.part_pad + lax.rem(j, self.part)


def lane_map(value, places, wide, dtype=BF16):
    shape = value.shape[:-1] + (wide,)
    flat = value.reshape(-1, value.shape[-1])
    rows = flat.shape[0]
    block = rows if rows % 256 else 256
    result = pl.pallas_call(
        functools.partial(lane_map_kernel, places),
        grid=(rows // block,),
        in_specs=[pl.BlockSpec((block, flat.shape[1]), lambda i: (i, 0))],
        out_specs=pl.BlockSpec((block, wide), lambda i: (i, 0)),
        out_shape=jax.ShapeDtypeStruct((rows, wide), dtype),
        compiler_params=pltpu.CompilerParams(vmem_limit_bytes=32 * 2**20),
        cost_estimate=FREE,
        name="lane_map",
    )(flat)
    return result.reshape(shape)


NT = (((1,), (1,)), ((), ()))
TN = (((0,), (0,)), ((), ()))
FREE = pl.CostEstimate(flops=0, bytes_accessed=0, transcendentals=0)


def on_each_part(info_ref, parts, body):
    if parts == 1:
        body(0)
        return
    for part in range(parts):
        pl.when(info_ref[info_ref.shape[0] - 1] == part)(functools.partial(body, part))


def heads_of_pair(body):
    if HL % 2 == 0:
        body((0, 1))
        return
    last = pl.program_id(1) == PAIRS - 1
    pl.when(jnp.logical_not(last))(functools.partial(body, (0, 1)))
    pl.when(last)(functools.partial(body, (0,)))


def attn_fwd_kernel(info_ref, q_ref, k_ref, v_ref, o_ref, lse_ref):
    total, rows = k_ref.shape[0], o_ref.shape[0]
    length = info_ref[pl.program_id(0)]
    block = min(ROW_BLOCK, rows)
    lower = lax.broadcasted_iota(jnp.int32, (block, 2 * HD), 1) < HD
    keep = jnp.where(lax.broadcasted_iota(jnp.int32, (total, 1), 0) < length, 0.0, -1e30)

    def body(heads, half):
        for i in range(rows // block):
            first = half * rows + i * block
            end = first + block
            key = lax.broadcasted_iota(jnp.int32, (end, block), 0)
            query = lax.broadcasted_iota(jnp.int32, (end, block), 1) + first
            probs = []
            for a in heads:
                mine = lower if a == 0 else jnp.logical_not(lower)
                q = jnp.where(mine, q_ref[first:end, :] * jnp.asarray(HD**-0.5, BF16), jnp.zeros((), BF16))
                scores = lax.dot_general(k_ref[:end, :], q, NT, preferred_element_type=F32) + keep[:end]
                scores = jnp.where(key <= query, scores, -1e30)
                top = jnp.max(scores, axis=0, keepdims=True)
                weights = jnp.exp(scores - top)
                below = jnp.sum(weights, axis=0, keepdims=True)
                lse_ref[a : a + 1, i * block : (i + 1) * block] = top + jnp.log(below)
                probs.append((weights * (1.0 / below)).astype(BF16))
            parts = [lax.dot_general(p, v_ref[:end, :], TN, preferred_element_type=F32) for p in probs]
            upper = parts[1] if len(heads) == 2 else jnp.zeros_like(parts[0])
            o_ref[i * block : (i + 1) * block, :] = jnp.where(lower, parts[0], upper).astype(BF16)

    lse_ref[...] = jnp.zeros_like(lse_ref)
    heads_of_pair(lambda heads: on_each_part(info_ref, total // rows, functools.partial(body, heads)))


def pair_spec(rows, lanes, offset=0):
    return pl.BlockSpec((None, rows, lanes), lambda i, j: (i, 0, j + offset))


def stats_spec(rows):
    return pl.BlockSpec((None, None, 2, rows), lambda i, j: (i, j, 0, 0))


def attn_forward(packed, info, rows):
    count, total, _ = packed.shape
    return pl.pallas_call(
        attn_fwd_kernel,
        grid=(count, PAIRS),
        in_specs=[
            pl.BlockSpec(memory_space=pltpu.SMEM),
            pair_spec(total, 2 * HD),
            pair_spec(total, 2 * HD, PAIRS),
            pair_spec(total, 2 * HD, 2 * PAIRS),
        ],
        out_specs=[pair_spec(rows, 2 * HD), stats_spec(rows)],
        out_shape=[
            jax.ShapeDtypeStruct((count, rows, V_LANES), BF16),
            jax.ShapeDtypeStruct((count, PAIRS, 2, rows), F32),
        ],
        compiler_params=pltpu.CompilerParams(vmem_limit_bytes=48 * 2**20),
        cost_estimate=FREE,
        name="attn_fwd",
    )(info, packed, packed, packed)


def attn_bwd_kernel(info_ref, q_ref, k_ref, v_ref, g_ref, o_ref, lse_ref, out_ref):
    total, rows = k_ref.shape[0], g_ref.shape[0]
    block = min(2 * ROW_BLOCK, rows)
    count = total // block
    pair = pl.program_id(1)
    length = info_ref[pl.program_id(0)]
    lane = lax.broadcasted_iota(jnp.int32, (block, 2 * HD), 1)
    key = lax.broadcasted_iota(jnp.int32, (block, block), 0)
    query = lax.broadcasted_iota(jnp.int32, (block, block), 1)
    key_row = lax.broadcasted_iota(jnp.int32, (block, 1), 0)

    def body(heads, half):
        nothing = jnp.zeros((block, 2 * HD), F32)
        dq, dk, dv = {}, {}, {}
        for i in range(rows // block):
            at = slice(i * block, (i + 1) * block)
            place = half * rows // block + i
            g = g_ref[at, :]
            product = g.astype(F32) * o_ref[at, :].astype(F32)
            mine = {}
            for a in heads:
                lanes = (lane < HD) if a == 0 else (lane >= HD)
                inner = lax.dot_general(
                    jnp.ones((8, 2 * HD), F32),
                    jnp.where(lanes, product, 0.0),
                    NT,
                    preferred_element_type=F32,
                    precision=lax.Precision.HIGHEST,
                )[0:1]
                q = q_ref[place * block : (place + 1) * block, :] * jnp.asarray(HD**-0.5, BF16)
                q = jnp.where(lanes, q, jnp.zeros_like(q))
                mine[a] = (q, jnp.where(lanes, g, jnp.zeros_like(g)), inner, lse_ref[a : a + 1, at])
            for j in range(place + 1):
                keys = slice(j * block, (j + 1) * block)
                keep = jnp.where(key_row < length - j * block, 0.0, -1e30)
                for a in heads:
                    q, g_mine, inner, lse = mine[a]
                    k = k_ref[keys, :]
                    scores = lax.dot_general(k, q, NT, preferred_element_type=F32) + keep
                    if j == place:
                        scores = jnp.where(key <= query, scores, -1e30)
                    probs = jnp.exp(scores - lse)
                    gprobs = lax.dot_general(v_ref[keys, :], g_mine, NT, preferred_element_type=F32)
                    gscores = (probs * (gprobs - inner)).astype(BF16)
                    dq[a, place] = dq.get((a, place), 0.0) + lax.dot_general(
                        gscores, k, TN, preferred_element_type=F32
                    )
                    dk[a, j] = dk.get((a, j), 0.0) + jnp.dot(gscores, q, preferred_element_type=F32)
                    dv[j] = dv.get(j, 0.0) + jnp.dot(probs.astype(BF16), g_mine, preferred_element_type=F32)
        for j in range(count):
            at = slice(j * block, (j + 1) * block)
            low, high = heads[0], heads[-1]
            dq_both = jnp.where(lane < HD, dq.get((low, j), nothing), dq.get((high, j), nothing)) * HD**-0.5
            dk_both = jnp.where(lane < HD, dk.get((low, j), nothing), dk.get((high, j), nothing))
            for which, value in enumerate((dq_both, dk_both, dv.get(j, nothing))):
                start = pl.multiple_of(which * V_LANES + pair * 2 * HD, 2 * HD)
                out_ref[at, pl.ds(start, 2 * HD)] = value.astype(BF16)

    heads_of_pair(lambda heads: on_each_part(info_ref, total // rows, functools.partial(body, heads)))


def attn_backward(packed, grad, attended, lse, info):
    (count, total, _), rows = packed.shape, grad.shape[1]
    return pl.pallas_call(
        attn_bwd_kernel,
        grid=(count, PAIRS),
        in_specs=[
            pl.BlockSpec(memory_space=pltpu.SMEM),
            pair_spec(total, 2 * HD),
            pair_spec(total, 2 * HD, PAIRS),
            pair_spec(total, 2 * HD, 2 * PAIRS),
            pair_spec(rows, 2 * HD),
            pair_spec(rows, 2 * HD),
            stats_spec(rows),
        ],
        out_specs=pl.BlockSpec((None, total, P_LANES), lambda i, j: (i, 0, 0)),
        out_shape=jax.ShapeDtypeStruct((count, total, P_LANES), BF16),
        compiler_params=pltpu.CompilerParams(vmem_limit_bytes=56 * 2**20),
        cost_estimate=FREE,
        name="attn_bwd",
    )(info, packed, packed, packed, grad, attended, lse)


PAIR = "x"


def flip(value, axis):
    return lax.ppermute(value, axis, [(0, 1), (1, 0)])


def in_turn(mine, other, mine_at, axis):
    shape = [1] * mine.ndim
    shape[axis] = 2
    place = lax.broadcasted_iota(jnp.int32, tuple(shape), axis)
    return jnp.where(place == mine_at, mine, other)


def pick(value, at, axis=0):
    return lax.dynamic_slice_in_dim(value, at, 1, axis=axis)


def there(*tokens):
    result = None
    for leaf in jax.tree.leaves(tokens):
        first = lax.slice(leaf, (0,) * leaf.ndim, (1,) * leaf.ndim).reshape(())
        result = (first == first) if result is None else result & (first == first)
    return result


def tied(value, *tokens):
    if not jax.tree.leaves(tokens):
        return value
    return value + jnp.where(there(tokens), 0, 1).astype(value.dtype)


def rows_of_both(own):
    count, rows, width = own.shape
    both = in_turn(own[:, None], flip(own, "section")[:, None], lax.axis_index("section"), 1)
    return both.reshape(count, 2 * rows, width)


def chip_rows(partial):
    count, rows, width = partial.shape
    core = lax.axis_index("section")
    split = partial.reshape(count, 2, rows // 2, width)
    other = flip(pick(split, 1 - core, 1)[:, 0], "section")
    return (pick(split, core, 1)[:, 0].astype(F32) + other.astype(F32)).astype(BF16)


class PairSum:
    def __init__(self):
        self.before = ()

    def hold(self, value):
        self.before += (value,)

    def __call__(self, chip):
        arrived = flip(tied(chip, self.before), PAIR)
        self.before = (arrived,)
        return chip.astype(F32) + arrived.astype(F32)


def dot(a, b):
    flat = jnp.dot(a.reshape(-1, a.shape[-1]), b, preferred_element_type=F32)
    return flat.reshape(a.shape[:-1] + (b.shape[1],))


def dot_t(a, b):
    flat = lax.dot_general(a.reshape(-1, a.shape[-1]), b, NT, preferred_element_type=F32)
    return flat.reshape(a.shape[:-1] + (b.shape[0],))


def dot_0(a, b):
    return lax.dot_general(a.reshape(-1, a.shape[-1]), b.reshape(-1, b.shape[-1]), TN, preferred_element_type=F32)


def row_sum(value):
    return jnp.sum(value.astype(F32), axis=(0, 1))


def gelu_parts(u):
    t = jnp.tanh(0.7978845608 * (u + 0.044715 * u * u * u))
    return t


def gelu(u):
    return 0.5 * u * (1.0 + gelu_parts(u))


def gelu_slope(u):
    t = gelu_parts(u)
    return 0.5 * (1.0 + t) + 0.5 * u * (1.0 - t * t) * 0.7978845608 * (1.0 + 3 * 0.044715 * u * u)


def norm_stats(rows, mask, width):
    average = jnp.sum(rows, axis=-1, keepdims=True) / width
    centered = (rows - average) * mask
    variance = jnp.sum(centered * centered, axis=-1, keepdims=True) / width
    scale = lax.rsqrt(variance + 1e-05)
    return centered * scale, scale


def norm_back(grad, rows, gain, mask, width):
    hat, scale = norm_stats(rows, mask, width)
    inner = grad * gain
    mean_one = jnp.sum(inner, axis=-1, keepdims=True) / width
    mean_two = jnp.sum(inner * hat, axis=-1, keepdims=True) / width
    back = scale * (inner - mean_one - hat * mean_two) * mask
    return back, row_sum(grad * hat), row_sum(grad * mask)


def whole_sequence(packed):
    parts = lax.axis_size("y")
    if parts == 2:
        other = lax.ppermute(packed[..., V_LANES:], "y", [(0, 1)])
        other = jnp.pad(other, ((0, 0), (0, 0), (V_LANES, 0)))
        both = in_turn(packed[:, None], other[:, None], lax.axis_index("y"), 1)
    else:
        both = lax.all_gather(packed, "y", axis=1)
    return both.reshape(packed.shape[0], parts * packed.shape[1], packed.shape[2])


def own_rows(grad):
    parts = lax.axis_size("y")
    rows = grad.shape[1] // parts
    if parts != 2:
        return lax.psum_scatter(grad, "y", scatter_dimension=1, tiled=True)
    other = lax.ppermute(grad[:, :rows, V_LANES:], "y", [(1, 0)])
    other = jnp.pad(other, ((0, 0), (0, 0), (V_LANES, 0)))
    own = lax.dynamic_slice_in_dim(grad, lax.axis_index("y") * rows, rows, axis=1)
    return (own.astype(F32) + other.astype(F32)).astype(BF16)


def project_stage(rows, w, mask, width):
    hat, _ = norm_stats(rows.astype(F32), mask, width)
    normed = rows_of_both((hat * w["gain_one"] + w["shift_one"]).astype(BF16))
    packed = (dot(normed, w["qkv"]) + w["qkv_bias"]).astype(BF16)
    return normed, whole_sequence(packed)


def attend_stage(normed, packed, w, info):
    attended, lse = attn_forward(packed, info, normed.shape[1])
    return dot(attended, w["out"]).astype(BF16), (normed, packed, attended, lse)


def ffn_stage(middle, w, mask, width):
    hat, _ = norm_stats(middle, mask, width)
    normed = rows_of_both((hat * w["gain_two"] + w["shift_two"]).astype(BF16))
    upward = dot(normed, w["up"]) + w["up_bias"]
    hidden = gelu(upward).astype(BF16)
    partial = dot(hidden, w["down"]).astype(BF16)
    return partial, (normed, upward.astype(BF16), hidden)


def ffn_back_stage(grad_out, kept, w, token=()):
    normed, upward, hidden = kept
    grad_down = tied(grad_out.astype(BF16), token)
    b_down = row_sum(grad_down)
    grad_down = rows_of_both(grad_down)
    grad_up = (dot_t(grad_down, w["down"]) * gelu_slope(upward.astype(F32))).astype(BF16)
    b_up = row_sum(grad_up)
    partial = dot_t(grad_up, w["up"]).astype(BF16)
    return partial, {"down_bias": b_down, "up_bias": b_up}, {"down": (hidden, grad_down), "up": (normed, grad_up)}


def branch_stage(grad_middle, kept, token=()):
    grad_branch = tied(grad_middle.astype(BF16), token)
    return rows_of_both(grad_branch), {"out_bias": row_sum(grad_branch)}


def attend_back_stage(grad_branch, kept, w, info):
    normed, packed, attended, lse = kept
    grad_attended = dot_t(grad_branch, w["out"]).astype(BF16)
    return attn_backward(packed, grad_attended, attended, lse, info)


def project_back_stage(grad_packed, kept, w):
    grad_packed = own_rows(grad_packed)
    b_packed = row_sum(grad_packed)
    partial = dot_t(grad_packed, w["qkv"]).astype(BF16)
    return partial, {"packed": b_packed}, {"qkv": (kept[0], grad_packed)}


SMALL = ("b_qv", "out_bias", "up_bias", "down_bias", "gain_one", "shift_one", "gain_two", "shift_two")


def per_device(
    inputs,
    cotangent,
    lengths,
    dealing,
    query_key_value_weight,
    b_qv,
    attention_out_weight,
    attention_out_bias,
    up_weight,
    up_bias,
    down_weight,
    down_bias,
    gain_one,
    shift_one,
    gain_two,
    shift_two,
):
    micro, block_rows, width = inputs.shape
    dp_count, y_count = lax.axis_size("dp"), lax.axis_size("y")
    chips = 2 * dp_count * y_count
    all_groups = dp_count * y_count
    core, dp_index = lax.axis_index("section"), lax.axis_index("dp")
    x_index, y_index = lax.axis_index("x"), lax.axis_index("y")
    quarter = 2 * x_index + core
    part = query_key_value_weight.shape[1]
    part_pad = round_up(part + 1, 8)
    width_pad = chips * part_pad
    hid = down_weight.shape[1] // 2
    hid_pad = round_up(hid, 8)
    while all_groups * hid_pad % 128:
        hid_pad += 8

    lane = lax.broadcasted_iota(jnp.int32, (1, width_pad), 1)
    mask = (lane % part_pad < part).astype(F32)
    local = lax.broadcasted_iota(jnp.int32, (V_LANES, width_pad), 0)
    column = lax.broadcasted_iota(jnp.int32, (V_LANES, width_pad), 1)
    whole_row = local + quarter * HSTEP * HD
    own_local = (local < HL * HD) & ((local >= HD) | (quarter == 0))
    placed = ((column == whole_row // part * part_pad + whole_row % part) & own_local).astype(BF16)
    side = round_up(width_pad // 2, 128)
    far = width_pad - side

    def widen(value):
        return lane_map(value, Spread(part, part_pad), width_pad)

    def narrow(value, dtype=BF16):
        return lane_map(value.astype(BF16), Gather(part, part_pad), width, dtype)

    def pad_rows(value, rows):
        return jnp.pad(value, ((0, rows - value.shape[0]), (0, 0)))

    small_in = dict(
        zip(SMALL, (b_qv, attention_out_bias, up_bias, down_bias, gain_one, shift_one, gain_two, shift_two))
    )
    small_sizes = {name: value.shape[1] for name, value in small_in.items()}
    small_row = jnp.concatenate([small_in[name][0] for name in SMALL])
    small_total = small_row.shape[0]

    shard = query_key_value_weight[0].reshape(part, 3, H, HD)

    out_wide = pad_rows(widen(attention_out_weight[0]), part_pad)
    out_pieces = jnp.stack([jnp.stack([out_wide[:, at : at + side]] * 2) for at in (0, far)])

    def attn_piece(q):
        from_head = HSTEP * q
        heads = shard[:, :, from_head : from_head + HL]
        body = jnp.pad(heads.reshape(part, 3, HL * HD), ((0, 0), (0, 0), (0, V_LANES - HL * HD)))
        body = body.reshape(part, P_LANES)
        row = jnp.pad(small_row, (0, P_LANES - small_total))[None]
        return pad_rows(jnp.concatenate([body, row], axis=0), part_pad)

    up_shard = up_weight[0].reshape(part, all_groups, 2, 2, hid)

    def up_piece(q):
        body = up_shard[:, :, q // 2, q % 2]
        body = jnp.pad(body, ((0, 0), (0, 0), (0, hid_pad - hid))).reshape(part, all_groups * hid_pad)
        return pad_rows(body, part_pad)

    attn_pieces = jnp.stack([jnp.stack([attn_piece(2 * x + c) for x in range(2)]) for c in range(2)])
    up_pieces = jnp.stack([jnp.stack([up_piece(2 * x + c) for x in range(2)]) for c in range(2)])
    down_wide = widen(down_weight[0]).reshape(2, hid, width_pad)
    down_pieces = jnp.pad(down_wide, ((0, 0), (0, hid_pad - hid), (0, 0)))

    def by_layer(pieces):
        mine, other = pick(pieces, core)[0], flip(pick(pieces, 1 - core)[0], "section")
        return [jnp.where(core == 0, mine, other), jnp.where(core == 0, other, mine)]

    def across_pair(pieces):
        both = in_turn(pick(pieces, x_index), flip(pick(pieces, 1 - x_index), PAIR), x_index, 0)
        return both.reshape(2 * part_pad, both.shape[-1])

    groups = ("dp", "y")
    down_l = by_layer(down_pieces)
    attn_l = [across_pair(pieces) for pieces in by_layer(jnp.concatenate([attn_pieces, out_pieces], axis=-1))]
    up_l = [across_pair(pieces) for pieces in by_layer(up_pieces)]
    def gather(piece, *tokens):
        return lax.all_gather(tied(piece, tokens), groups, axis=0)

    down_first, attn_first = gather(down_l[0]), gather(attn_l[0])
    up_first = gather(up_l[0], down_first)
    weights = []

    def layer_of(attn_all, up_all, down_all):
        if attn_all is None:
            return {"down": down_all.reshape(all_groups * hid_pad, width_pad)}
        if isinstance(attn_all, tuple):
            qkv_all, out_all = (piece.reshape(width_pad, -1) for piece in attn_all)
        else:
            attn_all = attn_all.reshape(width_pad, P_LANES + side)
            qkv_all, out_all = attn_all[:, :P_LANES], attn_all[:, P_LANES:]
        small_all = qkv_all.reshape(chips, part_pad, P_LANES)[:, part, :small_total]
        pieces, at = {}, 0
        for name in SMALL:
            pieces[name] = small_all[:, at : at + small_sizes[name]]
            at += small_sizes[name]

        def feature(name):
            return jnp.pad(pieces[name].astype(F32), ((0, 0), (0, part_pad - part))).reshape(1, width_pad)

        qv = pieces["b_qv"].astype(F32).reshape(2, H * HD)
        own_qv = lax.dynamic_slice_in_dim(qv, quarter * HSTEP * HD, HL * HD, axis=1)
        own_qv = jnp.pad(own_qv, ((0, 0), (0, V_LANES - HL * HD)))
        qkv_bias = jnp.concatenate([own_qv[0], jnp.zeros((V_LANES,), F32), own_qv[1]])[None]
        ups = pieces["up_bias"].astype(F32).reshape(all_groups, 2, 2, hid)
        up_mine = lax.dynamic_index_in_dim(
            lax.dynamic_index_in_dim(ups, x_index, 1, keepdims=False), core, 1, keepdims=False
        )
        up_bias_row = jnp.pad(up_mine, ((0, 0), (0, hid_pad - hid))).reshape(1, all_groups * hid_pad)
        sides = in_turn(out_all[None], flip(out_all, "section")[None], core, 0)
        out_both = jnp.concatenate([sides[0], sides[1, :, side - far :]], axis=1)
        out_mine = dot(placed, out_both).astype(BF16)
        return {
                "qkv": qkv_all.reshape(width_pad, P_LANES),
                "qkv_bias": qkv_bias,
                "out": out_mine,
                "out_bias": feature("out_bias"),
                "up": up_all.reshape(width_pad, all_groups * hid_pad),
                "up_bias": up_bias_row,
                "down": None if down_all is None else down_all.reshape(all_groups * hid_pad, width_pad),
                "down_bias": feature("down_bias"),
                "gain_one": feature("gain_one"),
                "shift_one": feature("shift_one"),
                "gain_two": feature("gain_two"),
                "shift_two": feature("shift_two"),
        }

    rounds = [range(0, micro - micro // 2), range(micro - micro // 2, micro)]
    turns = range(len(rounds))
    CORE_X = ("section", "x")

    def to_rounds(value):
        rows = jnp.where(core == x_index, value, lax.ppermute(value, CORE_X, [(0, 1), (3, 2)]))
        rows = widen(rows)
        return [rows[r.start : r.stop] for r in rounds]

    def to_blocks(value, layer):
        rows = narrow(jnp.concatenate(value, axis=0))
        pairs = [(0, 2 * layer), (3, 2 * layer + 1), (1, 2 - 2 * layer), (2, 3 - 2 * layer)]
        return lax.ppermute(rows, CORE_X, pairs)

    own_lengths = lax.dynamic_slice_in_dim(lengths, dp_index * micro, micro)
    positions = (2 * y_index + core) * block_rows + jnp.arange(block_rows, dtype=jnp.int32)
    turn_info = [jnp.concatenate([own_lengths[r.start : r.stop], y_index[None].astype(jnp.int32)]) for r in rounds]

    start_rows = to_rounds(inputs)
    grad_rows = to_rounds(tied(cotangent, up_first))

    kept_attn = [[None] * len(rounds) for _ in range(2)]
    kept_ffn = [[None] * len(rounds) for _ in range(2)]
    middles = [[None] * len(rounds) for _ in range(2)]
    entering = [start_rows, None]
    pair_sum = PairSum()
    outputs = [None, None]
    layers = [layer_of(attn_first, up_first, down_first), None]
    for l in range(2):
        w = layers[l]
        partials, chip = [None] * len(rounds), [None] * len(rounds)
        projected = [None] * len(rounds)
        for turn in reversed(turns):
            projected[turn] = project_stage(entering[l][turn], w, mask, width)
        if l == 0:
            out_second = gather(attn_l[1][:, P_LANES:], projected[0][1], up_first)
            qkv_second = gather(attn_l[1][:, :P_LANES], projected[0][1], up_first)
        else:
            weights.append(gather(down_l[1], projected[0][1]))
            layers[1].update(layer_of(None, None, weights[-1]))
        for turn in turns:
            partials[turn], kept_attn[l][turn] = attend_stage(*projected[turn], w, turn_info[turn])
        for turn in turns:
            middles[l][turn] = entering[l][turn].astype(F32) + pair_sum(chip_rows(partials[turn])) + w["out_bias"]
            partials[turn], kept_ffn[l][turn] = ffn_stage(middles[l][turn], w, mask, width)
            if l == 0 and turn == 0:
                up_second = gather(up_l[1], partials[turn])
                layers[1] = layer_of((qkv_second, out_second), up_second, None)
        outputs[l] = [
            (middles[l][turn] + pair_sum(chip_rows(partials[turn])) + w["down_bias"]).astype(BF16) for turn in turns
        ]
        if l == 0:
            entering[1] = outputs[0]

    def deal(token):
        acts_local = [to_blocks(outputs[l], l) for l in range(2)]
        acts_local = jnp.where(core == 0, acts_local[0], acts_local[1])
        total_seqs = dealing.shape[0]
        numbers = jnp.arange(total_seqs, dtype=jnp.int32)
        position = jnp.sum(jnp.where(dealing[:, None] == numbers[None, :], numbers[:, None], 0), axis=0)
        target = lax.dynamic_slice_in_dim(position, dp_index * micro, micro) // micro
        anchor = lax.dynamic_slice_in_dim(dealing, dp_index * micro, micro) // micro
        dealt = []
        for d in range(dp_count):
            dest = dp_index ^ d
            send = acts_local[0]
            for i in range(1, micro):
                send = jnp.where(target[i] == dest, acts_local[i], send)
            send = tied(send, token)
            if d:
                send = lax.ppermute(send, "dp", [(i, i ^ d) for i in range(dp_count)])
            dealt.append(send)
        result = []
        for j in range(micro):
            offset = anchor[j] ^ dp_index
            chosen = dealt[0]
            for d in range(1, dp_count):
                chosen = jnp.where(offset == d, dealt[d], chosen)
            result.append(chosen)
        return jnp.stack(result)

    def total(values):
        return functools.reduce(jnp.add, values)

    def product(operands):
        return total([dot_0(a, b) for a, b in operands]).astype(BF16)

    once = (x_index == 0).astype(F32)
    valid = [positions[None] < own_lengths[r.start : r.stop, None] for r in rounds]
    grads = [jnp.where(valid[turn][..., None], grad_rows[turn].astype(F32), 0.0) for turn in turns]

    def scattered(value, rows):
        value = value.reshape(all_groups, rows, value.shape[-1])
        return lax.psum_scatter(value, groups, scatter_dimension=0, tiled=False)

    finished = [None, None]
    small_rows = [None, None]
    token = ()
    sent_back = [None, None]
    for l in (1, 0):
        w = layers[l]
        smalls, operands, partials = [{} for _ in turns], [{} for _ in turns], [None] * len(rounds)
        for turn in turns:
            partials[turn], small, ops = ffn_back_stage(grads[turn], kept_ffn[l][turn], w, token)
            smalls[turn].update(small)
            operands[turn].update(ops)
        d_down = product([ops["down"] for ops in operands])
        d_up = product([ops["up"] for ops in operands])
        token = (d_down, d_up)
        down_done = scattered(d_down, hid_pad)
        up_done = scattered(d_up, 2 * part_pad)
        grad_middles = [None] * len(rounds)
        for turn in turns:
            if l == 0 and turn == 1:
                pair_sum.hold(finished[1]["up"])
            back, gain, shift = norm_back(
                pair_sum(chip_rows(partials[turn])), middles[l][turn], w["gain_two"], mask, width
            )
            smalls[turn].update({"gain_two": gain, "shift_two": shift})
            grad_middles[turn] = grads[turn] + back
        branches = [None] * len(rounds)
        for turn in turns:
            branches[turn], small = branch_stage(grad_middles[turn], kept_attn[l][turn], token)
            smalls[turn].update(small)
            operands[turn]["out"] = (kept_attn[l][turn][2], branches[turn])
        if l == 0:
            acts = deal(tuple(branches))
        d_out = dot_0(placed, product([ops["out"] for ops in operands])).astype(BF16)
        out_own = lax.dynamic_slice_in_dim(d_out, core * far, side, axis=1)
        out_other = flip(lax.dynamic_slice_in_dim(d_out, (1 - core) * far, side, axis=1), "section")
        d_out = (out_own.astype(F32) + out_other.astype(F32)).astype(BF16)
        out_done = scattered(d_out, 2 * part_pad)
        grad_packed, before = [None] * len(rounds), ()
        for turn in reversed(turns):
            grad_packed[turn] = attend_back_stage(
                branches[turn], kept_attn[l][turn], w, turn_info[turn] + jnp.where(there(before), 0, 1)
                if before
                else turn_info[turn]
            )
            before = (grad_packed[turn],)
        for turn in turns:
            partials[turn], small, ops = project_back_stage(grad_packed[turn], kept_attn[l][turn], w)
            smalls[turn].update(small)
            operands[turn].update(ops)
        d_qkv = product([ops["qkv"] for ops in operands])
        token = (d_qkv, out_done)
        qkv_done = scattered(d_qkv, 2 * part_pad)
        returned = []
        for turn in turns:
            if l == 1 and turn == 1:
                pair_sum.hold(down_done)
            if l == 0 and turn == 1:
                pair_sum.hold((acts, finished[1]["qkv"]))
            back, gain, shift = norm_back(
                pair_sum(chip_rows(partials[turn])), entering[l][turn].astype(F32), w["gain_one"], mask, width
            )
            smalls[turn].update({"gain_one": gain, "shift_one": shift})
            returned.append((grad_middles[turn] + back).astype(BF16))
        sent_back[l] = returned
        if l == 1:
            grads = [r.astype(F32) for r in returned]
        sums = {name: total([small[name] for small in smalls]) for name in smalls[0]}

        def feature_sum(name):
            return sums[name].reshape(chips, part_pad)[:, :part] * once

        own_head = (jnp.arange(HL * HD) >= HD) | (quarter == 0)
        q_sum = sums["packed"][: HL * HD]
        v_sum = sums["packed"][2 * V_LANES : 2 * V_LANES + HL * HD]
        qv_sum = jnp.stack(
            [
                lax.dynamic_update_slice_in_dim(
                    jnp.zeros((H * HD,), F32), jnp.where(own_head, s, 0.0), quarter * HSTEP * HD, axis=0
                )
                for s in (q_sum, v_sum)
            ]
        ).reshape(chips, -1)
        up_sum = sums["up_bias"].reshape(all_groups, 1, 1, hid_pad)[..., :hid]
        at_x = jnp.arange(2)[None, :, None, None] == x_index
        at_c = jnp.arange(2)[None, None, :, None] == core
        up_sum = jnp.where(at_x & at_c, up_sum, 0.0).reshape(chips, -1)
        small_cols = jnp.concatenate(
            [qv_sum, feature_sum("out_bias"), up_sum]
            + [feature_sum(name) for name in ("down_bias", "gain_one", "shift_one", "gain_two", "shift_two")],
            axis=1,
        ).astype(BF16)
        small_cols = jnp.pad(small_cols, ((0, 0), (0, P_LANES - small_total)))[:, None, :]
        small_rows[l] = small_cols.reshape(all_groups, 2, P_LANES)
        finished[l] = {"up": up_done, "down": down_done, "qkv": qkv_done, "out": out_done}

    small_done = jnp.concatenate(small_rows, axis=1).astype(F32)
    for axis in groups:
        count = lax.axis_size(axis)
        for bit in range((count - 1).bit_length()):
            small_done += lax.ppermute(small_done, axis, [(i, i ^ (1 << bit)) for i in range(count)])
    small_done = pick(small_done, dp_index * y_count + y_index).astype(BF16).reshape(2, 2, 1, P_LANES)
    spare = lax.broadcasted_iota(jnp.int32, (1, part_pad, 1), 1) == part
    for l in range(2):
        rows = finished[l]["qkv"].reshape(2, part_pad, P_LANES)
        finished[l]["qkv"] = jnp.where(spare, small_done[l], rows).reshape(2 * part_pad, P_LANES)

    def back_across_pair(value):
        value = value.reshape(2, part_pad, value.shape[-1])
        return in_turn(pick(value, x_index), flip(pick(value, 1 - x_index), PAIR), x_index, 0)

    def own_layer(first, second):
        mine = jnp.where(core == 0, first, second)
        other = flip(jnp.where(core == 0, second, first), "section")
        return [jnp.where(core == 0, mine, other), jnp.where(core == 0, other, mine)]

    up_c = own_layer(*[back_across_pair(finished[l]["up"]) for l in range(2)])
    down_c = own_layer(*[finished[l]["down"].reshape(hid_pad, width_pad) for l in range(2)])
    qkv_c = own_layer(*[back_across_pair(finished[l]["qkv"]) for l in range(2)])
    out_c = own_layer(
        *[jnp.sum(back_across_pair(finished[l]["out"]).astype(F32), axis=0).astype(BF16) for l in range(2)]
    )

    def heads_sum(lanes_of):
        parts = []
        for x in range(2):
            for c in range(2):
                q = 2 * x + c
                piece = lanes_of(qkv_c[c][x, :part].astype(F32))
                own = jnp.arange(HL * HD) >= (0 if q == 0 else HD)
                piece = jnp.where(own[None], piece, 0.0)
                parts.append(jnp.pad(piece, ((0, 0), (HSTEP * q * HD, (H - HL - HSTEP * q) * HD))))
        return total(parts)

    def third(which):
        return lambda piece: piece[:, which * V_LANES : which * V_LANES + HL * HD]

    grad_w_qkv = jnp.concatenate([heads_sum(third(which)) for which in range(3)], axis=1)
    grad_w_out = narrow(jnp.concatenate([out_c[0], out_c[1][:, side - far :]], axis=1), F32)[:part]
    up_parts = jnp.stack(
        [
            jnp.stack(
                [
                    up_c[c][x, :part].reshape(part, all_groups, hid_pad)[..., :hid] for c in range(2)
                ],
                axis=2,
            )
            for x in range(2)
        ],
        axis=2,
    )
    grad_w_up = up_parts.astype(F32).reshape(part, -1)
    grad_w_down = narrow(jnp.concatenate([down_c[0][:hid], down_c[1][:hid]], axis=0), F32)
    small_sum = total([qkv_c[c][x, part, :small_total].astype(F32) for x in range(2) for c in range(2)])
    small_out, at = {}, 0
    for name in SMALL:
        small_out[name] = small_sum[at : at + small_sizes[name]]
        at += small_sizes[name]

    grads_local = [to_blocks(sent_back[l], l) for l in range(2)]
    input_grad = jnp.where(core == 0, grads_local[0], grads_local[1])
    return (
        acts[None],
        input_grad[None],
        grad_w_qkv[None],
        small_out["b_qv"][None],
        grad_w_out[None],
        small_out["out_bias"][None],
        grad_w_up[None],
        small_out["up_bias"][None],
        grad_w_down[None],
        small_out["down_bias"][None],
        small_out["gain_one"][None],
        small_out["shift_one"][None],
        small_out["gain_two"][None],
        small_out["shift_two"][None],
    )


def solution(mesh):
    sections, groups, positions = (mesh.shape[name] for name in ("section", "dp", "seq"))
    devices = mesh.devices.reshape(sections, groups, positions // 2, 2)
    split = jax.sharding.Mesh(devices, ("section", "dp", "y", "x"))
    seq = ("y", "x")
    wide = P("section", ("dp",) + seq, None)
    thin = P("section", ("dp",) + seq)
    rows = P("dp", seq, None)
    in_specs = (rows, rows, P(), P()) + (wide, thin) * 4 + (thin,) * 4
    out_specs = (P("section", "dp", seq, None),) * 2 + (wide, thin) * 4 + (thin,) * 4
    return jax.shard_map(per_device, mesh=split, in_specs=in_specs, out_specs=out_specs, check_vma=False)
```
